512 devices in a mesh: gx: 64 (over y, x, z_lo), gy: 8 (over z_hi, core).
Axes of the slice: x: 4, y: 8, z: 8 (z_hi: 4, z_lo: 2; z = z_hi * 2 + z_lo), core: 2. Of those that a mesh axis runs over, the one named last changes fastest.
Arguments:
- droplet_mass: float32 [512, 33, 4, 1024], P('gx', None, None, 'gy'), may hold values from 0.05 to 1
- wind_x: float32 [512, 4, 1024], P('gx', None, 'gy'), may hold values from -0.35 to 0.35
- wind_y: float32 [512, 4, 1024], P('gx', None, 'gy'), may hold values from -0.35 to 0.35
- kernel: float32 [33, 33], replicated, may hold values from 0.01 to 0.08
- breakup: float32 [33, 33], replicated, may hold values from 0.05 to 0.6
- target: int32 [33, 33], replicated, may hold values from 1 to 32, as said below
- fragment_low: int32 [33, 33], replicated, may hold values from 0 to 32, as said below
- cloudy: int32 [512, 8], P('gx', 'gy'), may hold values from 0 to 1, as said below
Outputs:
- mass_out: float32 [512, 33, 4, 1024], P('gx', None, None, 'gy')
The draws below stay inside these ranges and needn't reach their ends.
Inputs may be any that keep to these rules, and one draw needn't show every extreme that they name: Of the 8 column blocks of one device, at most 4 are cloudy, and some device has exactly 4 cloudy blocks. target[i][j] is min(max(i, j) + 1, 32) or min(max(i, j) + 2, 32). fragment_low[i][j] lies between 0 and min(i, j).
All inputs are finite; a program needn't handle non-finite values.
Results may differ from the reference program's by a relative error of at most 0.00043.
Values sent between devices are 32-bit elements; how exact they have to be, the bound alone decides.
A program may use at most 64 MiB of HBM per device.

```python
import math
import jax
import jax.numpy as jnp
from jax import lax

BINS = 33
LEVELS = 4
CX = 8
CY = 128
STEPS = 2
CAP = 4
NX = 512
NY = 1024


def draw_target(key, part):
    first = lax.broadcasted_iota(jnp.int32, (BINS, BINS), 0)
    second = lax.broadcasted_iota(jnp.int32, (BINS, BINS), 1)
    offset = jax.random.randint(jax.random.fold_in(key, 11), (BINS, BINS), 1, 3)
    offset = jnp.where(first + second == 0, 1, offset)
    return jnp.minimum(jnp.maximum(first, second) + offset, BINS - 1).astype(jnp.int32)


def draw_fragment_low(key, part):
    first = lax.broadcasted_iota(jnp.int32, (BINS, BINS), 0)
    second = lax.broadcasted_iota(jnp.int32, (BINS, BINS), 1)
    raw = jax.random.randint(jax.random.fold_in(key, 23), (BINS, BINS), 0, 1 << 20)
    low = raw % (jnp.minimum(first, second) + 1)
    corner = (first == BINS - 1) & (second == BINS - 1)
    return jnp.where(corner, BINS - 1, low).astype(jnp.int32)


def draw_cloudy(key, part):
    tiles_x = NX // CX
    tiles_y = NY // CY
    tiles = tiles_x * tiles_y
    counts = jax.random.randint(jax.random.fold_in(key, 31), (tiles,), 0, CAP + 1)
    fullest = jax.random.randint(jax.random.fold_in(key, 37), (), 0, tiles)
    counts = jnp.where(jnp.arange(tiles, dtype=jnp.int32) == fullest, CAP, counts)
    scores = jax.random.randint(jax.random.fold_in(key, 41), (tiles, CX), 0, 1 << 20) * CX + jnp.arange(CX, dtype=jnp.int32)[None, :]
    ranks = jnp.argsort(jnp.argsort(scores, axis=-1), axis=-1)
    flags = (ranks < counts[:, None]).astype(jnp.int32)
    flags = flags.reshape(tiles_x, tiles_y, CX)
    return jnp.transpose(flags, (0, 2, 1)).reshape(NX, tiles_y).astype(jnp.int32)


def block_levels(rng, dims, pieces, low, largest):
    loudness = 1.0
    for position, parts in pieces:
        steps = jax.random.uniform(jax.random.fold_in(jax.random.fold_in(rng, 6), position), (parts,), jnp.float32, low / len(pieces), largest / len(pieces))
        loudness = loudness * jnp.repeat(jnp.exp(steps), dims[position] // parts).reshape((-1,) + (1,) * (len(dims) - 1 - position))
    return loudness


def setup_inputs(seed: int = 0) -> dict:
    key_of = jax.random.split(jax.random.key(seed), 9)
    return {
        "droplet_mass": jnp.clip(jnp.exp(math.log(1.0) - 2.9957323 * jax.random.uniform(key_of[0], (NX, BINS, LEVELS, NY), jnp.float32) ** block_levels(key_of[0], (NX, BINS, LEVELS, NY), ((0, 64), (3, 8)), -0.2, 0.2)), 0.05, 1.0),
        "wind_x": jnp.clip(jax.random.uniform(key_of[1], (NX, LEVELS, NY), jnp.float32, -0.35, 0.35) * block_levels(key_of[1], (NX, LEVELS, NY), ((0, 64), (2, 8)), -0.4, 0.0), -0.35, 0.35),
        "wind_y": jnp.clip(jax.random.uniform(key_of[2], (NX, LEVELS, NY), jnp.float32, -0.35, 0.35) * block_levels(key_of[2], (NX, LEVELS, NY), ((0, 64), (2, 8)), -0.4, 0.0), -0.35, 0.35),
        "kernel": jnp.clip(jnp.exp(jax.random.uniform(key_of[3], (BINS, BINS), jnp.float32, math.log(0.01), math.log(0.08))), 0.01, 0.08),
        "breakup": jnp.clip(jax.random.uniform(key_of[4], (BINS, BINS), jnp.float32, 0.05, 0.6), 0.05, 0.6),
        "target": draw_target(jax.random.fold_in(key_of[8], 71), 0),
        "fragment_low": draw_fragment_low(jax.random.fold_in(key_of[8], 71), 0),
        "cloudy": draw_cloudy(jax.random.fold_in(key_of[8], 71), 0),
    }


def upwind(courant, behind, behind_two, ahead, ahead_two):
    return jnp.maximum(courant, 0.0) * (1.5 * behind - 0.5 * behind_two) + jnp.minimum(courant, 0.0) * (1.5 * ahead - 0.5 * ahead_two)


def advect_rate(field, faces_x, faces_y):
    flux_x = upwind(faces_x, jnp.roll(field, 1, 0), jnp.roll(field, 2, 0), field, jnp.roll(field, -1, 0))
    flux_y = upwind(faces_y, jnp.roll(field, 1, 3), jnp.roll(field, 2, 3), field, jnp.roll(field, -1, 3))
    return -(jnp.roll(flux_x, -1, 0) - flux_x) - (jnp.roll(flux_y, -1, 3) - flux_y)


def collision_matrix(kernel, breakup, target, fragment_low):
    count = kernel.shape[0]
    first = lax.broadcasted_iota(jnp.int32, (count, count), 0)
    second = lax.broadcasted_iota(jnp.int32, (count, count), 1)
    larger = jnp.maximum(first, second)
    spread = (larger - fragment_low + 1).astype(jnp.float32)
    levels = jnp.arange(count, dtype=jnp.int32)[:, None, None]
    merged = (levels == target[None]).astype(jnp.float32)
    broken = ((levels >= fragment_low[None]) & (levels <= larger[None])).astype(jnp.float32) / spread[None]
    losses = 0.5 * ((levels == first[None]).astype(jnp.float32) + (levels == second[None]).astype(jnp.float32))
    portion = (1.0 - breakup)[None] * merged + breakup[None] * broken - losses
    return (kernel[None] * portion).reshape(count, count * count).astype(jnp.bfloat16)


def collide(field, matrix, cloudy):
    width_x, count, depth, width_y = field.shape
    tiles_y = cloudy.shape[1]
    block_y = width_y // tiles_y
    tiles = (width_x // CX) * tiles_y
    total = width_x * tiles_y
    flags = cloudy.reshape(total)
    order = jnp.argsort((1 - flags) * total + jnp.arange(total, dtype=jnp.int32))
    chosen = order[:tiles * CAP]
    live = flags[chosen].astype(jnp.float32)
    rows_x = chosen // tiles_y
    rows_t = chosen % tiles_y
    shaped = field.reshape(width_x, count, depth, tiles_y, block_y)
    blocks = shaped[rows_x, :, :, rows_t, :]
    group = 16 * CAP
    picked = blocks.reshape(tiles * CAP // group, group, count, depth * block_y)

    def one_group(piece):
        cells = jnp.transpose(piece, (1, 0, 2)).reshape(count, -1)
        products = (cells[:, None, :] * cells[None, :, :]).reshape(count * count, -1)
        products = lax.optimization_barrier(products.astype(jnp.bfloat16)).astype(jnp.float32)
        change = jnp.dot(matrix, products, preferred_element_type=jnp.float32)
        return jnp.transpose(change.reshape(count, group, depth * block_y), (1, 0, 2))

    change = lax.map(one_group, picked).reshape(tiles * CAP, count, depth, block_y)
    shaped = shaped.at[rows_x, :, :, rows_t, :].add(change * live[:, None, None, None])
    return shaped.reshape(width_x, count, depth, width_y)


def reference(droplet_mass, wind_x, wind_y, kernel, breakup, target, fragment_low, cloudy):
    matrix = collision_matrix(kernel, breakup, target, fragment_low)
    matrix = lax.optimization_barrier(matrix).astype(jnp.float32)
    faces_x = jnp.roll(wind_x, 1, 0)[:, None]
    faces_y = jnp.roll(wind_y, 1, 2)[:, None]
    state = droplet_mass
    for repeat in range(STEPS):
        first = state + advect_rate(state, faces_x, faces_y)
        state = 0.5 * state + 0.5 * (first + advect_rate(first, faces_x, faces_y))
        state = collide(state, matrix, cloudy)
    return state
```

```python
import functools

import jax
import jax.numpy as jnp
from jax import lax
from jax.experimental import pallas as pl
from jax.experimental.pallas import tpu as pltpu
from jax.sharding import PartitionSpec as P

STEPS = 2
STAGES = 2 * STEPS
BINS = 33
MAIN = 32
LEVELS = 4
CX = 8
CY = 128
CAP = 4
DEPTH = 688
ROWS = 48
EDGE = 2 * MAIN + CX
MESH = pl.DeviceIdType.MESH


def pair_pieces():
    pieces = []
    for a in range(8):
        pieces.append((32 * a, a, 0, 32))
        pieces.append((32 * (8 + a), 24 + a, 24, 32))
        pieces.append((32 * (8 + a) + 8, 8 + a, 8, 32))
    for a in range(4):
        pieces.append((32 * (16 + a), 20 + a, 16, 32))
        pieces.append((32 * (16 + a) + 16, 16 + a, 16, 32))
    pieces.append((32 * 20, 32, 0, 32))
    pieces.append((32 * 21, 32, 32, 33))
    return pieces


def build_matrix(tables, padded, flipped, parts, matrix):
    for n, table in enumerate(tables):
        padded[n] = jnp.zeros((128, 128), jnp.float32)
        padded[n, 0:BINS, 0:BINS] = table[...].astype(jnp.float32)
        flipped[n] = padded[n].T
    out_bin = lax.broadcasted_iota(jnp.int32, (ROWS, 128), 0).astype(jnp.float32)
    second = lax.broadcasted_iota(jnp.int32, (ROWS, 128), 1)
    lanes = lax.broadcasted_iota(jnp.int32, (1, 128), 1)

    def one(i, carry):
        first = jnp.full((1, 128), i, jnp.int32).astype(jnp.float32)
        larger = jnp.maximum(first, lanes.astype(jnp.float32))
        losses = 0.5 * jnp.where(out_bin == first, 1.0, 0.0) + 0.5 * jnp.where(
            out_bin == second.astype(jnp.float32), 1.0, 0.0
        )

        def rates(source):
            kern, brk, tgt, low = (source[n, pl.ds(i, 1), :] for n in range(4))
            each = brk * (1.0 / (larger - low + 1.0))
            merged = jnp.where(out_bin == tgt, 1.0 - brk, 0.0)
            broken = jnp.where((out_bin >= low) & (out_bin <= larger), each, 0.0)
            rounded = (kern * (merged + broken - losses)).astype(jnp.bfloat16)
            return rounded.astype(jnp.float32)

        start = jnp.where(i == MAIN, 0, (i // 8) * 8 + 8)
        end = jnp.where(i == MAIN, MAIN, BINS)
        both = (second >= start) & (second < end)
        parts[i] = rates(padded) + jnp.where(both, rates(flipped), 0.0)
        return carry

    lax.fori_loop(0, BINS, one, 0)
    for tile in range(0, DEPTH, 128):
        acc = jnp.zeros((ROWS, 128), jnp.float32)
        for place, i, low, high in pair_pieces():
            at = place - tile
            if 0 <= at < 128:
                moved = pltpu.roll(parts[i], (at - low) % 128, 1)
                acc = jnp.where((second >= at) & (second < at + high - low), moved, acc)
        width = min(128, DEPTH - tile)
        high = acc.astype(jnp.bfloat16)
        rest = (acc - high.astype(jnp.float32)).astype(jnp.bfloat16)
        matrix[0:ROWS, tile : tile + width] = high[:, :width]
        matrix[ROWS : 2 * ROWS, tile : tile + width] = rest[:, :width]


def kernel(
    size_x,
    size_y,
    mass,
    wind_x,
    wind_y,
    table_kernel,
    table_breakup,
    table_target,
    table_low,
    cloudy,
    out,
    state,
    last,
    moved,
    moved_last,
    coef,
    send_x,
    send_y,
    got_x,
    got_y,
    got_wx,
    got_wy,
    padded,
    flipped,
    parts,
    matrix,
    products,
    change,
    sem_sx,
    sem_rx,
    sem_sy,
    sem_ry,
    sem_sw,
    sem_rw,
):
    gx = lax.axis_index("gx")
    gy = lax.axis_index("gy")
    west = (lax.rem(gx + size_x - 1, size_x), gy)
    east = (lax.rem(gx + 1, size_x), gy)
    south = (gx, lax.rem(gy + size_y - 1, size_y))
    north = (gx, lax.rem(gy + 1, size_y))
    lane = lax.broadcasted_iota(jnp.int32, (CX, CY), 1)
    row = lax.broadcasted_iota(jnp.int32, (CX, CY), 0)
    wide = lax.broadcasted_iota(jnp.int32, (MAIN, CY), 1)

    def remote(src, dst, send, recv, device):
        return pltpu.make_async_remote_copy(
            src_ref=src, dst_ref=dst, send_sem=send, recv_sem=recv, device_id=device, device_id_type=MESH
        )

    def copies(stage, level):
        out = []
        for side, device in ((0, west), (1, east)):
            out.append(
                remote(
                    send_x.at[stage, level, side],
                    got_x.at[stage, level, 1 - side],
                    sem_sx.at[stage, level, side],
                    sem_rx.at[stage, level, 1 - side],
                    device,
                )
            )
        for side, device in ((0, south), (1, north)):
            out.append(
                remote(
                    send_y.at[stage, level],
                    got_y.at[stage, level, 1 - side],
                    sem_sy.at[stage, level, side],
                    sem_ry.at[stage, level, 1 - side],
                    device,
                )
            )
        return out

    def wind_copies():
        return [
            remote(wind_x.at[pl.ds(24, 8)], got_wx, sem_sw.at[0], sem_rw.at[0], east),
            remote(wind_y, got_wy, sem_sw.at[1], sem_rw.at[1], north),
        ]

    def keep(stage, level, values, tail):
        pack = jnp.zeros((CX, CY), jnp.float32)
        for x in range(CX):
            value = values(x)
            state[stage, level, x] = value
            if x < 2:
                send_x[stage, level, 0, x * MAIN : (x + 1) * MAIN] = value
            if x >= CX - 2:
                at = x - (CX - 2)
                send_x[stage, level, 1, at * MAIN : (at + 1) * MAIN] = value
            for j in range(4):
                at = 32 * j + 4 * x
                turned = pltpu.roll(value[8 * j : 8 * j + 8], (at - 126) % 128, 1)
                pack = jnp.where((lane >= at) & (lane < at + 4), turned, pack)
        send_x[stage, level, 0, 2 * MAIN : EDGE] = tail
        send_x[stage, level, 1, 2 * MAIN : EDGE] = tail
        send_y[stage, level, 0:CX] = pack
        send_y[stage, level, CX : 2 * CX] = tail

    barrier = pltpu.get_barrier_semaphore()
    for device in (west, east, south, north):
        pl.semaphore_signal(barrier, inc=1, device_id=device, device_id_type=MESH)

    def load(level, carry):
        tail = mass[pl.ds(4 * MAIN + level, CX, stride=4 * BINS), :]
        last[0, level] = tail
        keep(0, level, lambda x: mass[pl.ds(x * 4 * BINS + level, MAIN, stride=4), :], tail)
        return carry

    lax.fori_loop(0, LEVELS, load, 0)
    pl.semaphore_wait(barrier, 4)
    for copy in wind_copies():
        copy.start()

    def send_first(level, carry):
        for copy in copies(0, level):
            copy.start()
        return carry

    lax.fori_loop(0, LEVELS, send_first, 0)

    build_matrix((table_kernel, table_breakup, table_target, table_low), padded, flipped, parts, matrix)

    flags = [cloudy[x, 0] for x in range(CX)]
    count = jnp.int32(0)
    chosen = [jnp.int32(0)] * CAP
    slots = []
    for x in range(CX):
        slots.append(jnp.minimum(count, CAP - 1))
        for r in range(CAP):
            chosen[r] = jnp.where((flags[x] > 0) & (count == r), x, chosen[r])
        count = count + flags[x]
    live = [flags[x].astype(jnp.float32) for x in range(CX)]

    for copy in wind_copies():
        copy.wait_recv()

    def coefficients(level, carry):
        right = wind_x[pl.ds(level, CX, stride=LEVELS), :]
        left = jnp.where(row == 0, got_wx[pl.ds(4 + level, 1), :], pltpu.roll(right, 1, 0))
        above = wind_y[pl.ds(level, CX, stride=LEVELS), :]
        ghost = got_wy[pl.ds(level, CX, stride=LEVELS), :]
        below = pltpu.roll(jnp.where(lane == CY - 1, ghost, above), 1, 1)

        def five(low, high):
            plus_low, minus_low = jnp.maximum(low, 0.0), jnp.minimum(low, 0.0)
            plus_high, minus_high = jnp.maximum(high, 0.0), jnp.minimum(high, 0.0)
            return (
                -0.5 * plus_low,
                1.5 * plus_low + 0.5 * plus_high,
                1.5 * minus_low - 1.5 * plus_high,
                -0.5 * minus_low - 1.5 * minus_high,
                0.5 * minus_high,
            )

        in_x = five(left, right)
        in_y = five(below, above)
        for n, value in enumerate(
            (in_x[0], in_x[1], in_x[3], in_x[4], in_y[0], in_y[1], in_y[3], in_y[4], 1.0 + (in_x[2] + in_y[2]))
        ):
            coef[level, n] = value
        return carry

    lax.fori_loop(0, LEVELS, coefficients, 0)

    def advance(stage, level):
        edge = jnp.where(lax.rem(lane, 4) < 2, got_y[stage, level, 0, 0:CX], got_y[stage, level, 1, 0:CX])

        def at_x(x):
            if x < 0:
                return got_x[stage, level, 0, (x + 2) * MAIN : (x + 3) * MAIN]
            if x >= CX:
                return got_x[stage, level, 1, (x - CX) * MAIN : (x - CX + 1) * MAIN]
            return state[stage, level, x]

        def value(x):
            c = [coef[level, n, x : x + 1, :] for n in range(9)]
            q = at_x(x)
            acc = c[8] * q
            acc += c[0] * at_x(x - 2) + c[1] * at_x(x - 1)
            acc += c[2] * at_x(x + 1) + c[3] * at_x(x + 2)
            ends = jnp.concatenate(
                [pltpu.roll(edge, (126 - 32 * j - 4 * x) % 128, 1) for j in range(4)], axis=0
            )
            acc += c[4] * pltpu.roll(jnp.where(wide >= CY - 2, ends, q), 2, 1)
            acc += c[5] * pltpu.roll(jnp.where(wide >= CY - 1, ends, q), 1, 1)
            acc += c[6] * pltpu.roll(jnp.where(wide < 1, ends, q), CY - 1, 1)
            acc += c[7] * pltpu.roll(jnp.where(wide < 2, ends, q), CY - 2, 1)
            return acc

        c = [coef[level, n] for n in range(9)]
        e = last[stage, level]
        below_x = got_x[stage, level, 0, 2 * MAIN : EDGE]
        above_x = got_x[stage, level, 1, 2 * MAIN : EDGE]
        below_y = got_y[stage, level, 0, CX : 2 * CX]
        above_y = got_y[stage, level, 1, CX : 2 * CX]
        acc = c[8] * e
        acc += c[0] * pltpu.roll(jnp.where(row >= CX - 2, below_x, e), 2, 0)
        acc += c[1] * pltpu.roll(jnp.where(row >= CX - 1, below_x, e), 1, 0)
        acc += c[2] * pltpu.roll(jnp.where(row < 1, above_x, e), CX - 1, 0)
        acc += c[3] * pltpu.roll(jnp.where(row < 2, above_x, e), CX - 2, 0)
        acc += c[4] * pltpu.roll(jnp.where(lane >= CY - 2, below_y, e), 2, 1)
        acc += c[5] * pltpu.roll(jnp.where(lane >= CY - 1, below_y, e), 1, 1)
        acc += c[6] * pltpu.roll(jnp.where(lane < 1, above_y, e), CY - 1, 1)
        acc += c[7] * pltpu.roll(jnp.where(lane < 2, above_y, e), CY - 2, 1)
        return value, acc

    def collide():
        for r in range(CAP):
            x = chosen[r]
            cols = slice(r * CY, (r + 1) * CY)
            n = moved[x]
            e = moved_last[pl.ds(x, 1), :]

            def bin_of(i):
                return moved[x, i : i + 1, :]

            for a in range(8):
                products[32 * a : 32 * a + 32, cols] = (bin_of(a) * n).astype(jnp.bfloat16)
                products[32 * (8 + a) : 32 * (9 + a), cols] = jnp.concatenate(
                    [bin_of(24 + a) * n[24:32], bin_of(8 + a) * n[8:32]], axis=0
                ).astype(jnp.bfloat16)
            for a in range(4):
                products[32 * (16 + a) : 32 * (17 + a), cols] = jnp.concatenate(
                    [bin_of(20 + a) * n[16:32], bin_of(16 + a) * n[16:32]], axis=0
                ).astype(jnp.bfloat16)
            products[640:672, cols] = (e * n).astype(jnp.bfloat16)
            products[672:688, cols] = jnp.broadcast_to(e * e, (16, CY)).astype(jnp.bfloat16)
        result = jnp.dot(matrix[...], products[...], preferred_element_type=jnp.float32)
        for r in range(CAP):
            cols = slice(r * CY, (r + 1) * CY)
            change[r] = result[0:ROWS, cols] + result[ROWS : 2 * ROWS, cols]

    for stage in range(STAGES):

        def step(level, carry, stage=stage):
            for copy in copies(stage, level):
                copy.wait_recv()
            value, tail = advance(stage, level)
            if stage % 2 == 0:
                last[stage + 1, level] = tail
                keep(stage + 1, level, value, tail)
            else:
                for x in range(CX):
                    moved[x] = 0.5 * state[stage - 1, level, x] + 0.5 * value(x)
                moved_last[...] = 0.5 * last[stage - 1, level] + 0.5 * tail
                collide()

                def after(x):
                    return moved[x] + live[x] * change[slots[x], 0:MAIN]

                for x in range(CX):
                    moved_last[x : x + 1, :] = (
                        moved_last[x : x + 1, :] + live[x] * change[slots[x], MAIN : MAIN + 1]
                    )
                tail = moved_last[...]
                if stage < STAGES - 1:
                    last[stage + 1, level] = tail
                    keep(stage + 1, level, after, tail)
                else:
                    for x in range(CX):
                        out[pl.ds(x * 4 * BINS + level, MAIN, stride=4), :] = after(x)
                    out[pl.ds(4 * MAIN + level, CX, stride=4 * BINS), :] = tail
            if stage < STAGES - 1:
                for copy in copies(stage + 1, level):
                    copy.start()
            return carry

        lax.fori_loop(0, LEVELS, step, 0)

    for copy in wind_copies():
        copy.wait_send()
    for stage in range(STAGES):

        def finish(level, carry, stage=stage):
            for copy in copies(stage, level):
                copy.wait_send()
            return carry

        lax.fori_loop(0, LEVELS, finish, 0)


def local(size_x, size_y, droplet_mass, wind_x, wind_y, table, breakup, target, fragment_low, cloudy):
    vmem = pl.BlockSpec(memory_space=pltpu.VMEM)
    f32 = jnp.float32
    result = pl.pallas_call(
        functools.partial(kernel, size_x, size_y),
        out_shape=jax.ShapeDtypeStruct((CX * BINS * LEVELS, CY), f32),
        in_specs=[vmem] * 7 + [pl.BlockSpec(memory_space=pltpu.SMEM)],
        out_specs=vmem,
        scratch_shapes=[
            pltpu.VMEM((STAGES, LEVELS, CX, MAIN, CY), f32),
            pltpu.VMEM((STAGES, LEVELS, CX, CY), f32),
            pltpu.VMEM((CX, MAIN, CY), f32),
            pltpu.VMEM((CX, CY), f32),
            pltpu.VMEM((LEVELS, 9, CX, CY), f32),
            pltpu.VMEM((STAGES, LEVELS, 2, EDGE, CY), f32),
            pltpu.VMEM((STAGES, LEVELS, 2 * CX, CY), f32),
            pltpu.VMEM((STAGES, LEVELS, 2, EDGE, CY), f32),
            pltpu.VMEM((STAGES, LEVELS, 2, 2 * CX, CY), f32),
            pltpu.VMEM((8, CY), f32),
            pltpu.VMEM((CX * LEVELS, CY), f32),
            pltpu.VMEM((4, 128, 128), f32),
            pltpu.VMEM((4, 128, 128), f32),
            pltpu.VMEM((BINS, ROWS, 128), f32),
            pltpu.VMEM((2 * ROWS, DEPTH), jnp.bfloat16),
            pltpu.VMEM((DEPTH, CAP * CY), jnp.bfloat16),
            pltpu.VMEM((CAP, ROWS, CY), f32),
            pltpu.SemaphoreType.DMA((STAGES, LEVELS, 2)),
            pltpu.SemaphoreType.DMA((STAGES, LEVELS, 2)),
            pltpu.SemaphoreType.DMA((STAGES, LEVELS, 2)),
            pltpu.SemaphoreType.DMA((STAGES, LEVELS, 2)),
            pltpu.SemaphoreType.DMA((2,)),
            pltpu.SemaphoreType.DMA((2,)),
        ],
        compiler_params=pltpu.CompilerParams(
            collective_id=0, has_side_effects=True, vmem_limit_bytes=40 * 2**20
        ),
    )(
        droplet_mass.reshape(CX * BINS * LEVELS, CY),
        wind_x.reshape(CX * LEVELS, CY),
        wind_y.reshape(CX * LEVELS, CY),
        table,
        breakup,
        target,
        fragment_low,
        cloudy,
    )
    return result.reshape(CX, BINS, LEVELS, CY)


def solution(mesh):
    in_specs = (
        P("gx", None, None, "gy"),
        P("gx", None, "gy"),
        P("gx", None, "gy"),
        P(),
        P(),
        P(),
        P(),
        P("gx", "gy"),
    )
    return jax.shard_map(
        functools.partial(local, mesh.shape["gx"], mesh.shape["gy"]),
        mesh=mesh,
        in_specs=in_specs,
        out_specs=P("gx", None, None, "gy"),
        check_vma=False,
    )
```

```python
import functools

import jax
import jax.numpy as jnp
from jax import lax
from jax.experimental import pallas as pl
from jax.experimental.pallas import tpu as pltpu
from jax.sharding import PartitionSpec as P

STEPS = 2
STAGES = 2 * STEPS
BINS = 33
MAIN = 32
LEVELS = 4
CX = 8
CY = 128
CAP = 4
DEPTH = 688
ROWS = 48
EDGE = 2 * MAIN + 2
OUTER = (0, 1, CX - 2, CX - 1)
INNER = tuple(range(2, CX - 2))
MESH = pl.DeviceIdType.MESH


def pair_pieces():
    pieces = []
    for a in range(8):
        pieces.append((32 * a, a, 0, 32))
        pieces.append((32 * (8 + a), 24 + a, 24, 32))
        pieces.append((32 * (8 + a) + 8, 8 + a, 8, 32))
    for a in range(4):
        pieces.append((32 * (16 + a), 20 + a, 16, 32))
        pieces.append((32 * (16 + a) + 16, 16 + a, 16, 32))
    pieces.append((32 * 20, 32, 0, 32))
    pieces.append((32 * 21, 32, 32, 33))
    return pieces


def build_matrix(tables, padded, flipped, parts, matrix):
    for n, table in enumerate(tables):
        padded[n] = jnp.zeros((128, 128), jnp.float32)
        padded[n, 0:BINS, 0:BINS] = table[...].astype(jnp.float32)
        flipped[n] = padded[n].T
    out_bin = lax.broadcasted_iota(jnp.int32, (ROWS, 128), 0).astype(jnp.float32)
    second = lax.broadcasted_iota(jnp.int32, (ROWS, 128), 1)
    lanes = lax.broadcasted_iota(jnp.int32, (1, 128), 1)

    def one(i, carry):
        first = jnp.full((1, 128), i, jnp.int32).astype(jnp.float32)
        larger = jnp.maximum(first, lanes.astype(jnp.float32))
        losses = 0.5 * jnp.where(out_bin == first, 1.0, 0.0) + 0.5 * jnp.where(
            out_bin == second.astype(jnp.float32), 1.0, 0.0
        )

        def rates(source):
            kern, brk, tgt, low = (source[n, pl.ds(i, 1), :] for n in range(4))
            each = brk * (1.0 / (larger - low + 1.0))
            merged = jnp.where(out_bin == tgt, 1.0 - brk, 0.0)
            broken = jnp.where((out_bin >= low) & (out_bin <= larger), each, 0.0)
            rounded = (kern * (merged + broken - losses)).astype(jnp.bfloat16)
            return rounded.astype(jnp.float32)

        start = jnp.where(i == MAIN, 0, (i // 8) * 8 + 8)
        end = jnp.where(i == MAIN, MAIN, BINS)
        both = (second >= start) & (second < end)
        parts[i] = rates(padded) + jnp.where(both, rates(flipped), 0.0)
        return carry

    lax.fori_loop(0, BINS, one, 0)
    for tile in range(0, DEPTH, 128):
        acc = jnp.zeros((ROWS, 128), jnp.float32)
        for place, i, low, high in pair_pieces():
            at = place - tile
            if 0 <= at < 128:
                moved = pltpu.roll(parts[i], (at - low) % 128, 1)
                acc = jnp.where((second >= at) & (second < at + high - low), moved, acc)
        width = min(128, DEPTH - tile)
        high = acc.astype(jnp.bfloat16)
        rest = (acc - high.astype(jnp.float32)).astype(jnp.bfloat16)
        matrix[0:ROWS, tile : tile + width] = high[:, :width]
        matrix[ROWS : 2 * ROWS, tile : tile + width] = rest[:, :width]


def kernel(
    size_x,
    size_y,
    mass_in,
    wind_x_in,
    wind_y_in,
    table_kernel,
    table_breakup,
    table_target,
    table_low,
    cloudy_in,
    out,
    mass,
    wind_x,
    wind_y,
    tables_f,
    tables_i,
    cloudy,
    state,
    last,
    moved,
    moved_last,
    coef,
    send_x,
    send_y,
    got_x,
    got_y,
    got_wx,
    got_wy,
    send_wy,
    padded,
    flipped,
    parts,
    matrix,
    products,
    change,
    sem_sx,
    sem_rx,
    sem_sy,
    sem_ry,
    sem_sw,
    sem_rw,
    sem_in,
):
    gx = lax.axis_index("gx")
    gy = lax.axis_index("gy")
    west = (lax.rem(gx + size_x - 1, size_x), gy)
    east = (lax.rem(gx + 1, size_x), gy)
    south = (gx, lax.rem(gy + size_y - 1, size_y))
    north = (gx, lax.rem(gy + 1, size_y))
    lane = lax.broadcasted_iota(jnp.int32, (CX, CY), 1)
    row = lax.broadcasted_iota(jnp.int32, (CX, CY), 0)
    wide = lax.broadcasted_iota(jnp.int32, (MAIN, CY), 1)

    def remote(src, dst, send, recv, device):
        return pltpu.make_async_remote_copy(
            src_ref=src, dst_ref=dst, send_sem=send, recv_sem=recv, device_id=device, device_id_type=MESH
        )

    def copies_x(stage, level):
        out = []
        far = lax.rem(gx, 2)
        for side in (far, 1 - far):
            device = (lax.rem(gx + size_x - 1 + 2 * side, size_x), gy)
            out.append(
                remote(
                    send_x.at[stage, level, side],
                    got_x.at[stage, level, 1 - side],
                    sem_sx.at[stage, level, side],
                    sem_rx.at[stage, level, 1 - side],
                    device,
                )
            )
        return out

    def copies_y(stage, level):
        out = []
        for side, device in ((1, north), (0, south)):
            out.append(
                remote(
                    send_y.at[stage, level, side],
                    got_y.at[stage, level, 1 - side],
                    sem_sy.at[stage, level, side],
                    sem_ry.at[stage, level, 1 - side],
                    device,
                )
            )
        return out

    def copies(stage, level):
        return copies_x(stage, level) + copies_y(stage, level)

    def wind_copies():
        return [
            remote(wind_x_in.at[pl.ds(24, 8)], got_wx, sem_sw.at[0], sem_rw.at[0], east),
            remote(send_wy, got_wy, sem_sw.at[1], sem_rw.at[1], north),
        ]

    def packed(pack, x, value):
        for j in range(4):
            at = 32 * j + 4 * x
            turned = pltpu.roll(value[8 * j : 8 * j + 8], (at - 126) % 128, 1)
            pack = jnp.where((lane >= at) & (lane < at + 4), turned, pack)
        return pack

    def keep_row(stage, level, x, value):
        state[stage, level, x] = value
        if x in OUTER:
            side, at = (0, x) if x < 2 else (1, x - (CX - 2))
            send_x[stage, level, side, at * MAIN : (at + 1) * MAIN] = value

    def keep_y(stage, level, pack, tail):
        send_y[stage, level, 0] = jnp.where(lane < 2, tail, pack)
        send_y[stage, level, 1] = jnp.where((lane >= 2) & (lane < 4), pltpu.roll(tail, 4, 1), pack)

    def keep(stage, level, values, tail):
        pack = jnp.zeros((CX, CY), jnp.float32)
        last[stage, level] = tail
        send_x[stage, level, 0, 2 * MAIN : EDGE] = tail[0:2]
        send_x[stage, level, 1, 2 * MAIN : EDGE] = tail[CX - 2 : CX]
        for x in OUTER:
            value = values(x)
            keep_row(stage, level, x, value)
            pack = packed(pack, x, value)
        for x in INNER:
            value = values(x)
            keep_row(stage, level, x, value)
            pack = packed(pack, x, value)
        keep_y(stage, level, pack, tail)
        for copy in copies_y(stage, level) + copies_x(stage, level):
            copy.start()

    barrier = pltpu.get_barrier_semaphore()
    for device in (west, east, south, north):
        pl.semaphore_signal(barrier, inc=1, device_id=device, device_id_type=MESH)

    span = BINS * LEVELS

    def rows_in(low, high, n):
        rows = pl.ds(low * span, (high - low) * span)
        return pltpu.make_async_copy(mass_in.at[rows], mass.at[rows], sem_in.at[n])

    mass_copies = [rows_in(0, 2, 0), rows_in(CX - 2, CX, 1), rows_in(2, CX - 2, 2)]
    others = [
        pltpu.make_async_copy(src, dst, sem_in.at[3 + n])
        for n, (src, dst) in enumerate(
            (
                (wind_x_in, wind_x),
                (wind_y_in, wind_y),
                (table_kernel, tables_f.at[0]),
                (table_breakup, tables_f.at[1]),
                (table_target, tables_i.at[0]),
                (table_low, tables_i.at[1]),
                (cloudy_in, cloudy),
            )
        )
    ]
    for copy in mass_copies + others:
        copy.start()
    for copy in mass_copies[:2]:
        copy.wait()

    def load_outer(level, carry):
        for x in OUTER:
            side, at = (0, x) if x < 2 else (1, x - (CX - 2))
            keep_row(0, level, x, mass[pl.ds(x * span + level, MAIN, stride=4), :])
            send_x[0, level, side, 2 * MAIN + at : 2 * MAIN + at + 1] = mass[pl.ds(x * span + 4 * MAIN + level, 1), :]
        return carry

    lax.fori_loop(0, LEVELS, load_outer, 0)

    mass_copies[2].wait()

    def load_inner(level, carry):
        pack = jnp.zeros((CX, CY), jnp.float32)
        for x in INNER:
            keep_row(0, level, x, mass[pl.ds(x * span + level, MAIN, stride=4), :])
        for x in range(CX):
            pack = packed(pack, x, state[0, level, x])
        tail = mass[pl.ds(4 * MAIN + level, CX, stride=span), :]
        last[0, level] = tail
        keep_y(0, level, pack, tail)
        return carry

    lax.fori_loop(0, LEVELS, load_inner, 0)
    others[1].wait()
    wind_pack = jnp.zeros((CX, CY), jnp.float32)
    for level in range(LEVELS):
        turned = wind_y[pl.ds(level, CX, stride=LEVELS), :]
        wind_pack = jnp.where(lane == CY - 1 - level, pltpu.roll(turned, (CY - level) % CY, 1), wind_pack)
    send_wy[...] = wind_pack
    pl.semaphore_wait(barrier, 4)
    for copy in wind_copies():
        copy.start()
    def send_first_y(level, carry):
        for copy in copies_y(0, level):
            copy.start()
        return carry

    lax.fori_loop(0, LEVELS, send_first_y, 0)
    def send_first(level, carry):
        for copy in copies_x(0, level):
            copy.start()
        return carry

    lax.fori_loop(0, LEVELS, send_first, 0)
    for copy in others[:1] + others[2:]:
        copy.wait()
    build_matrix((tables_f.at[0], tables_f.at[1], tables_i.at[0], tables_i.at[1]), padded, flipped, parts, matrix)

    flags = [cloudy[0, x] for x in range(CX)]
    count = jnp.int32(0)
    chosen = [jnp.int32(0)] * CAP
    slots = []
    for x in range(CX):
        slots.append(jnp.minimum(count, CAP - 1))
        for r in range(CAP):
            chosen[r] = jnp.where((flags[x] > 0) & (count == r), x, chosen[r])
        count = count + flags[x]
    live = [flags[x].astype(jnp.float32) for x in range(CX)]

    for copy in wind_copies():
        copy.wait_recv()

    def coefficients(level, carry):
        right = wind_x[pl.ds(level, CX, stride=LEVELS), :]
        left = jnp.where(row == 0, got_wx[pl.ds(4 + level, 1), :], pltpu.roll(right, 1, 0))
        above = wind_y[pl.ds(level, CX, stride=LEVELS), :]
        ghost = pltpu.roll(got_wy[...], level, 1)
        below = pltpu.roll(jnp.where(lane == CY - 1, ghost, above), 1, 1)

        def five(low, high):
            plus_low, minus_low = jnp.maximum(low, 0.0), jnp.minimum(low, 0.0)
            plus_high, minus_high = jnp.maximum(high, 0.0), jnp.minimum(high, 0.0)
            return (
                -0.5 * plus_low,
                1.5 * plus_low + 0.5 * plus_high,
                1.5 * minus_low - 1.5 * plus_high,
                -0.5 * minus_low - 1.5 * minus_high,
                0.5 * minus_high,
            )

        in_x = five(left, right)
        in_y = five(below, above)
        for n, value in enumerate(
            (in_x[0], in_x[1], in_x[3], in_x[4], in_y[0], in_y[1], in_y[3], in_y[4], 1.0 + (in_x[2] + in_y[2]))
        ):
            coef[level, n] = value
        return carry

    lax.fori_loop(0, LEVELS, coefficients, 0)

    def advance(stage, level):
        edge = jnp.where(lax.rem(lane, 4) < 2, got_y[stage, level, 0], got_y[stage, level, 1])

        def at_x(x):
            if x < 0:
                return got_x[stage, level, 0, (x + 2) * MAIN : (x + 3) * MAIN]
            if x >= CX:
                return got_x[stage, level, 1, (x - CX) * MAIN : (x - CX + 1) * MAIN]
            return state[stage, level, x]

        def value(x):
            c = [coef[level, n, x : x + 1, :] for n in range(9)]
            q = at_x(x)
            acc = c[8] * q
            acc += c[0] * at_x(x - 2) + c[1] * at_x(x - 1)
            acc += c[2] * at_x(x + 1) + c[3] * at_x(x + 2)
            ends = jnp.concatenate(
                [pltpu.roll(edge, (126 - 32 * j - 4 * x) % 128, 1) for j in range(4)], axis=0
            )
            acc += c[4] * pltpu.roll(jnp.where(wide >= CY - 2, ends, q), 2, 1)
            acc += c[5] * pltpu.roll(jnp.where(wide >= CY - 1, ends, q), 1, 1)
            acc += c[6] * pltpu.roll(jnp.where(wide < 1, ends, q), CY - 1, 1)
            acc += c[7] * pltpu.roll(jnp.where(wide < 2, ends, q), CY - 2, 1)
            return acc

        c = [coef[level, n] for n in range(9)]
        e = last[stage, level]
        below_x = jnp.where(
            row == CX - 1,
            got_x[stage, level, 0, 2 * MAIN + 1 : 2 * MAIN + 2],
            got_x[stage, level, 0, 2 * MAIN : 2 * MAIN + 1],
        )
        above_x = jnp.where(
            row == 0,
            got_x[stage, level, 1, 2 * MAIN : 2 * MAIN + 1],
            got_x[stage, level, 1, 2 * MAIN + 1 : 2 * MAIN + 2],
        )
        below_y = pltpu.roll(got_y[stage, level, 0], CY - 4, 1)
        above_y = got_y[stage, level, 1]
        acc = c[8] * e
        acc += c[0] * pltpu.roll(jnp.where(row >= CX - 2, below_x, e), 2, 0)
        acc += c[1] * pltpu.roll(jnp.where(row >= CX - 1, below_x, e), 1, 0)
        acc += c[2] * pltpu.roll(jnp.where(row < 1, above_x, e), CX - 1, 0)
        acc += c[3] * pltpu.roll(jnp.where(row < 2, above_x, e), CX - 2, 0)
        acc += c[4] * pltpu.roll(jnp.where(lane >= CY - 2, below_y, e), 2, 1)
        acc += c[5] * pltpu.roll(jnp.where(lane >= CY - 1, below_y, e), 1, 1)
        acc += c[6] * pltpu.roll(jnp.where(lane < 1, above_y, e), CY - 1, 1)
        acc += c[7] * pltpu.roll(jnp.where(lane < 2, above_y, e), CY - 2, 1)
        return value, acc

    def collide():
        for r in range(CAP):
            x = chosen[r]
            cols = slice(r * CY, (r + 1) * CY)
            n = moved[x]
            e = moved_last[pl.ds(x, 1), :]

            def bin_of(i):
                return moved[x, i : i + 1, :]

            for a in range(8):
                products[32 * a : 32 * a + 32, cols] = (bin_of(a) * n).astype(jnp.bfloat16)
                products[32 * (8 + a) : 32 * (9 + a), cols] = jnp.concatenate(
                    [bin_of(24 + a) * n[24:32], bin_of(8 + a) * n[8:32]], axis=0
                ).astype(jnp.bfloat16)
            for a in range(4):
                products[32 * (16 + a) : 32 * (17 + a), cols] = jnp.concatenate(
                    [bin_of(20 + a) * n[16:32], bin_of(16 + a) * n[16:32]], axis=0
                ).astype(jnp.bfloat16)
            products[640:672, cols] = (e * n).astype(jnp.bfloat16)
            products[672:688, cols] = jnp.broadcast_to(e * e, (16, CY)).astype(jnp.bfloat16)
        result = jnp.dot(matrix[...], products[...], preferred_element_type=jnp.float32)
        for r in range(CAP):
            cols = slice(r * CY, (r + 1) * CY)
            change[r] = result[0:ROWS, cols] + result[ROWS : 2 * ROWS, cols]

    for stage in range(STAGES):

        def step(level, carry, stage=stage):
            for copy in copies(stage, level):
                copy.wait_recv()
            value, tail = advance(stage, level)
            if stage % 2 == 0:
                keep(stage + 1, level, value, tail)
            else:
                for x in range(CX):
                    moved[x] = 0.5 * state[stage - 1, level, x] + 0.5 * value(x)
                moved_last[...] = 0.5 * last[stage - 1, level] + 0.5 * tail
                collide()

                def after(x):
                    return moved[x] + live[x] * change[slots[x], 0:MAIN]

                for x in range(CX):
                    moved_last[x : x + 1, :] = (
                        moved_last[x : x + 1, :] + live[x] * change[slots[x], MAIN : MAIN + 1]
                    )
                tail = moved_last[...]
                if stage < STAGES - 1:
                    keep(stage + 1, level, after, tail)
                else:
                    for x in range(CX):
                        out[pl.ds(x * 4 * BINS + level, MAIN, stride=4), :] = after(x)
                    out[pl.ds(4 * MAIN + level, CX, stride=4 * BINS), :] = tail
            return carry

        lax.fori_loop(0, LEVELS, step, 0)

    for copy in wind_copies():
        copy.wait_send()
    for stage in range(STAGES):

        def finish(level, carry, stage=stage):
            for copy in copies(stage, level):
                copy.wait_send()
            return carry

        lax.fori_loop(0, LEVELS, finish, 0)


def local(size_x, size_y, droplet_mass, wind_x, wind_y, table, breakup, target, fragment_low, cloudy):
    vmem = pl.BlockSpec(memory_space=pltpu.VMEM)
    f32 = jnp.float32
    result = pl.pallas_call(
        functools.partial(kernel, size_x, size_y),
        out_shape=jax.ShapeDtypeStruct((CX * BINS * LEVELS, CY), f32),
        in_specs=[pl.BlockSpec(memory_space=pltpu.HBM)] * 8,
        out_specs=vmem,
        scratch_shapes=[
            pltpu.VMEM((CX * BINS * LEVELS, CY), f32),
            pltpu.VMEM((CX * LEVELS, CY), f32),
            pltpu.VMEM((CX * LEVELS, CY), f32),
            pltpu.VMEM((2, BINS, BINS), f32),
            pltpu.VMEM((2, BINS, BINS), jnp.int32),
            pltpu.SMEM((1, CX), jnp.int32),
            pltpu.VMEM((STAGES, LEVELS, CX, MAIN, CY), f32),
            pltpu.VMEM((STAGES, LEVELS, CX, CY), f32),
            pltpu.VMEM((CX, MAIN, CY), f32),
            pltpu.VMEM((CX, CY), f32),
            pltpu.VMEM((LEVELS, 9, CX, CY), f32),
            pltpu.VMEM((STAGES, LEVELS, 2, EDGE, CY), f32),
            pltpu.VMEM((STAGES, LEVELS, 2, CX, CY), f32),
            pltpu.VMEM((STAGES, LEVELS, 2, EDGE, CY), f32),
            pltpu.VMEM((STAGES, LEVELS, 2, CX, CY), f32),
            pltpu.VMEM((8, CY), f32),
            pltpu.VMEM((CX, CY), f32),
            pltpu.VMEM((CX, CY), f32),
            pltpu.VMEM((4, 128, 128), f32),
            pltpu.VMEM((4, 128, 128), f32),
            pltpu.VMEM((BINS, ROWS, 128), f32),
            pltpu.VMEM((2 * ROWS, DEPTH), jnp.bfloat16),
            pltpu.VMEM((DEPTH, CAP * CY), jnp.bfloat16),
            pltpu.VMEM((CAP, ROWS, CY), f32),
            pltpu.SemaphoreType.DMA((STAGES, LEVELS, 2)),
            pltpu.SemaphoreType.DMA((STAGES, LEVELS, 2)),
            pltpu.SemaphoreType.DMA((STAGES, LEVELS, 2)),
            pltpu.SemaphoreType.DMA((STAGES, LEVELS, 2)),
            pltpu.SemaphoreType.DMA((2,)),
            pltpu.SemaphoreType.DMA((2,)),
            pltpu.SemaphoreType.DMA((10,)),
        ],
        compiler_params=pltpu.CompilerParams(
            collective_id=0, has_side_effects=True, vmem_limit_bytes=62 * 2**20
        ),
    )(
        droplet_mass.reshape(CX * BINS * LEVELS, CY),
        wind_x.reshape(CX * LEVELS, CY),
        wind_y.reshape(CX * LEVELS, CY),
        table,
        breakup,
        target,
        fragment_low,
        cloudy.reshape(1, CX),
    )
    return result.reshape(CX, BINS, LEVELS, CY)


def solution(mesh):
    in_specs = (
        P("gx", None, None, "gy"),
        P("gx", None, "gy"),
        P("gx", None, "gy"),
        P(),
        P(),
        P(),
        P(),
        P("gx", "gy"),
    )
    return jax.shard_map(
        functools.partial(local, mesh.shape["gx"], mesh.shape["gy"]),
        mesh=mesh,
        in_specs=in_specs,
        out_specs=P("gx", None, None, "gy"),
        check_vma=False,
    )
```

```python
import functools

import jax
import jax.numpy as jnp
from jax import lax
from jax.experimental import pallas as pl
from jax.experimental.pallas import tpu as pltpu
from jax.sharding import PartitionSpec as P

STEPS = 2
STAGES = 2 * STEPS
BINS = 33
MAIN = 32
LEVELS = 4
CX = 8
CY = 128
CAP = 4
DEPTH = 688
ROWS = 48
EDGE = 2 * MAIN + 2
OUTER = (0, 1, CX - 2, CX - 1)
INNER = tuple(range(2, CX - 2))
MESH = pl.DeviceIdType.MESH


def pair_pieces():
    pieces = []
    for a in range(8):
        pieces.append((32 * a, a, 0, 32))
        pieces.append((32 * (8 + a), 24 + a, 24, 32))
        pieces.append((32 * (8 + a) + 8, 8 + a, 8, 32))
    for a in range(4):
        pieces.append((32 * (16 + a), 20 + a, 16, 32))
        pieces.append((32 * (16 + a) + 16, 16 + a, 16, 32))
    pieces.append((32 * 20, 32, 0, 32))
    pieces.append((32 * 21, 32, 32, 33))
    return pieces


def build_matrix(tables, padded, flipped, parts, matrix):
    for n, table in enumerate(tables):
        padded[n] = jnp.zeros((128, 128), jnp.float32)
        padded[n, 0:BINS, 0:BINS] = table[...].astype(jnp.float32)
        flipped[n] = padded[n].T
    out_bin = lax.broadcasted_iota(jnp.int32, (ROWS, 128), 0).astype(jnp.float32)
    second = lax.broadcasted_iota(jnp.int32, (ROWS, 128), 1)
    lanes = lax.broadcasted_iota(jnp.int32, (1, 128), 1)

    def one(i, carry):
        first = jnp.full((1, 128), i, jnp.int32).astype(jnp.float32)
        larger = jnp.maximum(first, lanes.astype(jnp.float32))
        losses = 0.5 * jnp.where(out_bin == first, 1.0, 0.0) + 0.5 * jnp.where(
            out_bin == second.astype(jnp.float32), 1.0, 0.0
        )

        def rates(source):
            kern, brk, tgt, low = (source[n, pl.ds(i, 1), :] for n in range(4))
            each = brk * (1.0 / (larger - low + 1.0))
            merged = jnp.where(out_bin == tgt, 1.0 - brk, 0.0)
            broken = jnp.where((out_bin >= low) & (out_bin <= larger), each, 0.0)
            rounded = (kern * (merged + broken - losses)).astype(jnp.bfloat16)
            return rounded.astype(jnp.float32)

        start = jnp.where(i == MAIN, 0, (i // 8) * 8 + 8)
        end = jnp.where(i == MAIN, MAIN, BINS)
        both = (second >= start) & (second < end)
        parts[i] = rates(padded) + jnp.where(both, rates(flipped), 0.0)
        return carry

    lax.fori_loop(0, BINS, one, 0)
    for tile in range(0, DEPTH, 128):
        acc = jnp.zeros((ROWS, 128), jnp.float32)
        for place, i, low, high in pair_pieces():
            at = place - tile
            if 0 <= at < 128:
                moved = pltpu.roll(parts[i], (at - low) % 128, 1)
                acc = jnp.where((second >= at) & (second < at + high - low), moved, acc)
        width = min(128, DEPTH - tile)
        high = acc.astype(jnp.bfloat16)
        rest = (acc - high.astype(jnp.float32)).astype(jnp.bfloat16)
        matrix[0:ROWS, tile : tile + width] = high[:, :width]
        matrix[ROWS : 2 * ROWS, tile : tile + width] = rest[:, :width]


def kernel(
    size_x,
    size_y,
    mass_in,
    wind_x_in,
    wind_y_in,
    table_kernel,
    table_breakup,
    table_target,
    table_low,
    cloudy_in,
    out,
    mass,
    wind_x,
    wind_y,
    tables_f,
    tables_i,
    cloudy,
    state,
    last,
    moved,
    moved_last,
    coef,
    send_x,
    send_y,
    got_x,
    got_y,
    got_wx,
    got_wy,
    send_wy,
    padded,
    flipped,
    parts,
    matrix,
    products,
    change,
    sem_sx,
    sem_rx,
    sem_sy,
    sem_ry,
    sem_sw,
    sem_rw,
    sem_in,
):
    gx = lax.axis_index("gx")
    gy = lax.axis_index("gy")
    west = (lax.rem(gx + size_x - 1, size_x), gy)
    east = (lax.rem(gx + 1, size_x), gy)
    south = (gx, lax.rem(gy + size_y - 1, size_y))
    north = (gx, lax.rem(gy + 1, size_y))
    lane = lax.broadcasted_iota(jnp.int32, (CX, CY), 1)
    row = lax.broadcasted_iota(jnp.int32, (CX, CY), 0)
    wide = lax.broadcasted_iota(jnp.int32, (MAIN, CY), 1)

    def remote(src, dst, send, recv, device):
        return pltpu.make_async_remote_copy(
            src_ref=src, dst_ref=dst, send_sem=send, recv_sem=recv, device_id=device, device_id_type=MESH
        )

    def copies_x(stage, level):
        out = []
        far = lax.rem(gx, 2)
        for side in (far, 1 - far):
            device = (lax.rem(gx + size_x - 1 + 2 * side, size_x), gy)
            out.append(
                remote(
                    send_x.at[stage, level, side],
                    got_x.at[stage, level, 1 - side],
                    sem_sx.at[stage, level, side],
                    sem_rx.at[stage, level, 1 - side],
                    device,
                )
            )
        return out

    def copies_y(stage, level):
        out = []
        for side, device in ((1, north), (0, south)):
            out.append(
                remote(
                    send_y.at[stage, level, side],
                    got_y.at[stage, level, 1 - side],
                    sem_sy.at[stage, level, side],
                    sem_ry.at[stage, level, 1 - side],
                    device,
                )
            )
        return out

    def copies(stage, level):
        return copies_x(stage, level) + copies_y(stage, level)

    def wind_copies():
        return [
            remote(wind_x_in.at[pl.ds(24, 8)], got_wx, sem_sw.at[0], sem_rw.at[0], east),
            remote(send_wy, got_wy, sem_sw.at[1], sem_rw.at[1], north),
        ]

    def packed(pack, x, value):
        for j in range(4):
            at = 32 * j + 4 * x
            turned = pltpu.roll(value[8 * j : 8 * j + 8], (at - 126) % 128, 1)
            pack = jnp.where((lane >= at) & (lane < at + 4), turned, pack)
        return pack

    def keep_row(stage, level, x, value):
        state[stage, level, x] = value
        if x in OUTER:
            side, at = (0, x) if x < 2 else (1, x - (CX - 2))
            send_x[stage, level, side, at * MAIN : (at + 1) * MAIN] = value

    def keep_y(stage, level, pack, tail):
        send_y[stage, level, 0] = jnp.where(lane < 2, tail, pack)
        send_y[stage, level, 1] = jnp.where((lane >= 2) & (lane < 4), pltpu.roll(tail, 4, 1), pack)

    def keep(stage, level, values, tail):
        pack = jnp.zeros((CX, CY), jnp.float32)
        last[stage, level] = tail
        send_x[stage, level, 0, 2 * MAIN : EDGE] = tail[0:2]
        send_x[stage, level, 1, 2 * MAIN : EDGE] = tail[CX - 2 : CX]
        for x in OUTER:
            value = values(x)
            keep_row(stage, level, x, value)
            pack = packed(pack, x, value)
        for x in INNER:
            value = values(x)
            keep_row(stage, level, x, value)
            pack = packed(pack, x, value)
        keep_y(stage, level, pack, tail)
        for copy in copies_y(stage, level) + copies_x(stage, level):
            copy.start()

    barrier = pltpu.get_barrier_semaphore()
    for device in (west, east, south, north):
        pl.semaphore_signal(barrier, inc=1, device_id=device, device_id_type=MESH)

    span = BINS * LEVELS

    def rows_in(low, high, n):
        rows = pl.ds(low * span, (high - low) * span)
        return pltpu.make_async_copy(mass_in.at[rows], mass.at[rows], sem_in.at[n])

    mass_copies = [rows_in(0, 2, 0), rows_in(CX - 2, CX, 1), rows_in(2, CX - 2, 2)]
    others = [
        pltpu.make_async_copy(src, dst, sem_in.at[3 + n])
        for n, (src, dst) in enumerate(
            (
                (wind_x_in, wind_x),
                (wind_y_in, wind_y),
                (table_kernel, tables_f.at[0]),
                (table_breakup, tables_f.at[1]),
                (table_target, tables_i.at[0]),
                (table_low, tables_i.at[1]),
                (cloudy_in, cloudy),
            )
        )
    ]
    for copy in mass_copies + others:
        copy.start()
    for copy in mass_copies[:2]:
        copy.wait()

    def load_outer(level, carry):
        for x in OUTER:
            side, at = (0, x) if x < 2 else (1, x - (CX - 2))
            keep_row(0, level, x, mass[pl.ds(x * span + level, MAIN, stride=4), :])
            send_x[0, level, side, 2 * MAIN + at : 2 * MAIN + at + 1] = mass[pl.ds(x * span + 4 * MAIN + level, 1), :]
        return carry

    lax.fori_loop(0, LEVELS, load_outer, 0)

    others[1].wait()
    wind_pack = jnp.zeros((CX, CY), jnp.float32)
    for level in range(LEVELS):
        turned = wind_y[pl.ds(level, CX, stride=LEVELS), :]
        wind_pack = jnp.where(lane == CY - 1 - level, pltpu.roll(turned, (CY - level) % CY, 1), wind_pack)
    send_wy[...] = wind_pack
    pl.semaphore_wait(barrier, 4)
    for copy in wind_copies():
        copy.start()
    mass_copies[2].wait()

    def load_inner(level, carry):
        pack = jnp.zeros((CX, CY), jnp.float32)
        for x in INNER:
            keep_row(0, level, x, mass[pl.ds(x * span + level, MAIN, stride=4), :])
        for x in range(CX):
            pack = packed(pack, x, state[0, level, x])
        tail = mass[pl.ds(4 * MAIN + level, CX, stride=span), :]
        last[0, level] = tail
        keep_y(0, level, pack, tail)
        for copy in copies_y(0, level) + copies_x(0, level):
            copy.start()
        return carry

    lax.fori_loop(0, LEVELS, load_inner, 0)

    for copy in others[:1] + others[2:]:
        copy.wait()
    build_matrix((tables_f.at[0], tables_f.at[1], tables_i.at[0], tables_i.at[1]), padded, flipped, parts, matrix)

    flags = [cloudy[0, x] for x in range(CX)]
    count = jnp.int32(0)
    chosen = [jnp.int32(0)] * CAP
    slots = []
    for x in range(CX):
        slots.append(jnp.minimum(count, CAP - 1))
        for r in range(CAP):
            chosen[r] = jnp.where((flags[x] > 0) & (count == r), x, chosen[r])
        count = count + flags[x]
    live = [flags[x].astype(jnp.float32) for x in range(CX)]

    for copy in wind_copies():
        copy.wait_recv()

    def coefficients(level, carry):
        right = wind_x[pl.ds(level, CX, stride=LEVELS), :]
        left = jnp.where(row == 0, got_wx[pl.ds(4 + level, 1), :], pltpu.roll(right, 1, 0))
        above = wind_y[pl.ds(level, CX, stride=LEVELS), :]
        ghost = pltpu.roll(got_wy[...], level, 1)
        below = pltpu.roll(jnp.where(lane == CY - 1, ghost, above), 1, 1)

        def five(low, high):
            plus_low, minus_low = jnp.maximum(low, 0.0), jnp.minimum(low, 0.0)
            plus_high, minus_high = jnp.maximum(high, 0.0), jnp.minimum(high, 0.0)
            return (
                -0.5 * plus_low,
                1.5 * plus_low + 0.5 * plus_high,
                1.5 * minus_low - 1.5 * plus_high,
                -0.5 * minus_low - 1.5 * minus_high,
                0.5 * minus_high,
            )

        in_x = five(left, right)
        in_y = five(below, above)
        for n, value in enumerate(
            (in_x[0], in_x[1], in_x[3], in_x[4], in_y[0], in_y[1], in_y[3], in_y[4], 1.0 + (in_x[2] + in_y[2]))
        ):
            coef[level, n] = value
        return carry

    lax.fori_loop(0, LEVELS, coefficients, 0)

    def advance(stage, level):
        edge = jnp.where(lax.rem(lane, 4) < 2, got_y[stage, level, 0], got_y[stage, level, 1])

        def at_x(x):
            if x < 0:
                return got_x[stage, level, 0, (x + 2) * MAIN : (x + 3) * MAIN]
            if x >= CX:
                return got_x[stage, level, 1, (x - CX) * MAIN : (x - CX + 1) * MAIN]
            return state[stage, level, x]

        def value(x):
            c = [coef[level, n, x : x + 1, :] for n in range(9)]
            q = at_x(x)
            acc = c[8] * q
            acc += c[0] * at_x(x - 2) + c[1] * at_x(x - 1)
            acc += c[2] * at_x(x + 1) + c[3] * at_x(x + 2)
            ends = jnp.concatenate(
                [pltpu.roll(edge, (126 - 32 * j - 4 * x) % 128, 1) for j in range(4)], axis=0
            )
            acc += c[4] * pltpu.roll(jnp.where(wide >= CY - 2, ends, q), 2, 1)
            acc += c[5] * pltpu.roll(jnp.where(wide >= CY - 1, ends, q), 1, 1)
            acc += c[6] * pltpu.roll(jnp.where(wide < 1, ends, q), CY - 1, 1)
            acc += c[7] * pltpu.roll(jnp.where(wide < 2, ends, q), CY - 2, 1)
            return acc

        c = [coef[level, n] for n in range(9)]
        e = last[stage, level]
        below_x = jnp.where(
            row == CX - 1,
            got_x[stage, level, 0, 2 * MAIN + 1 : 2 * MAIN + 2],
            got_x[stage, level, 0, 2 * MAIN : 2 * MAIN + 1],
        )
        above_x = jnp.where(
            row == 0,
            got_x[stage, level, 1, 2 * MAIN : 2 * MAIN + 1],
            got_x[stage, level, 1, 2 * MAIN + 1 : 2 * MAIN + 2],
        )
        below_y = pltpu.roll(got_y[stage, level, 0], CY - 4, 1)
        above_y = got_y[stage, level, 1]
        acc = c[8] * e
        acc += c[0] * pltpu.roll(jnp.where(row >= CX - 2, below_x, e), 2, 0)
        acc += c[1] * pltpu.roll(jnp.where(row >= CX - 1, below_x, e), 1, 0)
        acc += c[2] * pltpu.roll(jnp.where(row < 1, above_x, e), CX - 1, 0)
        acc += c[3] * pltpu.roll(jnp.where(row < 2, above_x, e), CX - 2, 0)
        acc += c[4] * pltpu.roll(jnp.where(lane >= CY - 2, below_y, e), 2, 1)
        acc += c[5] * pltpu.roll(jnp.where(lane >= CY - 1, below_y, e), 1, 1)
        acc += c[6] * pltpu.roll(jnp.where(lane < 1, above_y, e), CY - 1, 1)
        acc += c[7] * pltpu.roll(jnp.where(lane < 2, above_y, e), CY - 2, 1)
        return value, acc

    def collide():
        for r in range(CAP):
            x = chosen[r]
            cols = slice(r * CY, (r + 1) * CY)
            n = moved[x]
            e = moved_last[pl.ds(x, 1), :]

            def bin_of(i):
                return moved[x, i : i + 1, :]

            for a in range(8):
                products[32 * a : 32 * a + 32, cols] = (bin_of(a) * n).astype(jnp.bfloat16)
                products[32 * (8 + a) : 32 * (9 + a), cols] = jnp.concatenate(
                    [bin_of(24 + a) * n[24:32], bin_of(8 + a) * n[8:32]], axis=0
                ).astype(jnp.bfloat16)
            for a in range(4):
                products[32 * (16 + a) : 32 * (17 + a), cols] = jnp.concatenate(
                    [bin_of(20 + a) * n[16:32], bin_of(16 + a) * n[16:32]], axis=0
                ).astype(jnp.bfloat16)
            products[640:672, cols] = (e * n).astype(jnp.bfloat16)
            products[672:688, cols] = jnp.broadcast_to(e * e, (16, CY)).astype(jnp.bfloat16)
        result = jnp.dot(matrix[...], products[...], preferred_element_type=jnp.float32)
        for r in range(CAP):
            cols = slice(r * CY, (r + 1) * CY)
            change[r] = result[0:ROWS, cols] + result[ROWS : 2 * ROWS, cols]

    for stage in range(STAGES):

        def step(level, carry, stage=stage):
            for copy in copies(stage, level):
                copy.wait_recv()
            value, tail = advance(stage, level)
            if stage % 2 == 0:
                keep(stage + 1, level, value, tail)
            else:
                for x in range(CX):
                    moved[x] = 0.5 * state[stage - 1, level, x] + 0.5 * value(x)
                moved_last[...] = 0.5 * last[stage - 1, level] + 0.5 * tail
                collide()

                def after(x):
                    return moved[x] + live[x] * change[slots[x], 0:MAIN]

                for x in range(CX):
                    moved_last[x : x + 1, :] = (
                        moved_last[x : x + 1, :] + live[x] * change[slots[x], MAIN : MAIN + 1]
                    )
                tail = moved_last[...]
                if stage < STAGES - 1:
                    keep(stage + 1, level, after, tail)
                else:
                    for x in range(CX):
                        out[pl.ds(x * 4 * BINS + level, MAIN, stride=4), :] = after(x)
                    out[pl.ds(4 * MAIN + level, CX, stride=4 * BINS), :] = tail
            return carry

        lax.fori_loop(0, LEVELS, step, 0)

    for copy in wind_copies():
        copy.wait_send()
    for stage in range(STAGES):

        def finish(level, carry, stage=stage):
            for copy in copies(stage, level):
                copy.wait_send()
            return carry

        lax.fori_loop(0, LEVELS, finish, 0)


def local(size_x, size_y, droplet_mass, wind_x, wind_y, table, breakup, target, fragment_low, cloudy):
    vmem = pl.BlockSpec(memory_space=pltpu.VMEM)
    f32 = jnp.float32
    result = pl.pallas_call(
        functools.partial(kernel, size_x, size_y),
        out_shape=pltpu.VMEM((CX * BINS * LEVELS, CY), f32),
        in_specs=[pl.BlockSpec(memory_space=pltpu.HBM)] * 8,
        out_specs=vmem,
        scratch_shapes=[
            pltpu.VMEM((CX * BINS * LEVELS, CY), f32),
            pltpu.VMEM((CX * LEVELS, CY), f32),
            pltpu.VMEM((CX * LEVELS, CY), f32),
            pltpu.VMEM((2, BINS, BINS), f32),
            pltpu.VMEM((2, BINS, BINS), jnp.int32),
            pltpu.SMEM((1, CX), jnp.int32),
            pltpu.VMEM((STAGES, LEVELS, CX, MAIN, CY), f32),
            pltpu.VMEM((STAGES, LEVELS, CX, CY), f32),
            pltpu.VMEM((CX, MAIN, CY), f32),
            pltpu.VMEM((CX, CY), f32),
            pltpu.VMEM((LEVELS, 9, CX, CY), f32),
            pltpu.VMEM((STAGES, LEVELS, 2, EDGE, CY), f32),
            pltpu.VMEM((STAGES, LEVELS, 2, CX, CY), f32),
            pltpu.VMEM((STAGES, LEVELS, 2, EDGE, CY), f32),
            pltpu.VMEM((STAGES, LEVELS, 2, CX, CY), f32),
            pltpu.VMEM((8, CY), f32),
            pltpu.VMEM((CX, CY), f32),
            pltpu.VMEM((CX, CY), f32),
            pltpu.VMEM((4, 128, 128), f32),
            pltpu.VMEM((4, 128, 128), f32),
            pltpu.VMEM((BINS, ROWS, 128), f32),
            pltpu.VMEM((2 * ROWS, DEPTH), jnp.bfloat16),
            pltpu.VMEM((DEPTH, CAP * CY), jnp.bfloat16),
            pltpu.VMEM((CAP, ROWS, CY), f32),
            pltpu.SemaphoreType.DMA((STAGES, LEVELS, 2)),
            pltpu.SemaphoreType.DMA((STAGES, LEVELS, 2)),
            pltpu.SemaphoreType.DMA((STAGES, LEVELS, 2)),
            pltpu.SemaphoreType.DMA((STAGES, LEVELS, 2)),
            pltpu.SemaphoreType.DMA((2,)),
            pltpu.SemaphoreType.DMA((2,)),
            pltpu.SemaphoreType.DMA((10,)),
        ],
        compiler_params=pltpu.CompilerParams(
            collective_id=0, has_side_effects=True, vmem_limit_bytes=58 * 2**20
        ),
    )(
        droplet_mass.reshape(CX * BINS * LEVELS, CY),
        wind_x.reshape(CX * LEVELS, CY),
        wind_y.reshape(CX * LEVELS, CY),
        table,
        breakup,
        target,
        fragment_low,
        cloudy.reshape(1, CX),
    )
    return result.reshape(CX, BINS, LEVELS, CY)


def solution(mesh):
    in_specs = (
        P("gx", None, None, "gy"),
        P("gx", None, "gy"),
        P("gx", None, "gy"),
        P(),
        P(),
        P(),
        P(),
        P("gx", "gy"),
    )
    return jax.shard_map(
        functools.partial(local, mesh.shape["gx"], mesh.shape["gy"]),
        mesh=mesh,
        in_specs=in_specs,
        out_specs=P("gx", None, None, "gy"),
        check_vma=False,
    )
```

```python
import functools

import jax
import jax.numpy as jnp
from jax import lax
from jax.experimental import pallas as pl
from jax.experimental.pallas import tpu as pltpu
from jax.sharding import PartitionSpec as P

STEPS = 2
STAGES = 2 * STEPS
BINS = 33
MAIN = 32
LEVELS = 4
CX = 8
CY = 128
CAP = 4
DEPTH = 688
ROWS = 48
EDGE = 2 * MAIN + 2
OUTER = (0, 1, CX - 2, CX - 1)
INNER = tuple(range(2, CX - 2))
MESH = pl.DeviceIdType.MESH


def pair_pieces():
    pieces = []
    for a in range(8):
        pieces.append((32 * a, a, 0, 32))
        pieces.append((32 * (8 + a), 24 + a, 24, 32))
        pieces.append((32 * (8 + a) + 8, 8 + a, 8, 32))
    for a in range(4):
        pieces.append((32 * (16 + a), 20 + a, 16, 32))
        pieces.append((32 * (16 + a) + 16, 16 + a, 16, 32))
    pieces.append((32 * 20, 32, 0, 32))
    pieces.append((32 * 21, 32, 32, 33))
    return pieces


def build_matrix(tables, padded, flipped, parts, matrix):
    for n, table in enumerate(tables):
        padded[n] = jnp.zeros((128, 128), jnp.float32)
        padded[n, 0:BINS, 0:BINS] = table[...].astype(jnp.float32)
        flipped[n] = padded[n].T
    out_bin = lax.broadcasted_iota(jnp.int32, (ROWS, 128), 0).astype(jnp.float32)
    second = lax.broadcasted_iota(jnp.int32, (ROWS, 128), 1)
    lanes = lax.broadcasted_iota(jnp.int32, (1, 128), 1)

    def one(i, carry):
        first = jnp.full((1, 128), i, jnp.int32).astype(jnp.float32)
        larger = jnp.maximum(first, lanes.astype(jnp.float32))
        losses = 0.5 * jnp.where(out_bin == first, 1.0, 0.0) + 0.5 * jnp.where(
            out_bin == second.astype(jnp.float32), 1.0, 0.0
        )

        def rates(source):
            kern, brk, tgt, low = (source[n, pl.ds(i, 1), :] for n in range(4))
            each = brk * (1.0 / (larger - low + 1.0))
            merged = jnp.where(out_bin == tgt, 1.0 - brk, 0.0)
            broken = jnp.where((out_bin >= low) & (out_bin <= larger), each, 0.0)
            rounded = (kern * (merged + broken - losses)).astype(jnp.bfloat16)
            return rounded.astype(jnp.float32)

        start = jnp.where(i == MAIN, 0, (i // 8) * 8 + 8)
        end = jnp.where(i == MAIN, MAIN, BINS)
        both = (second >= start) & (second < end)
        parts[i] = rates(padded) + jnp.where(both, rates(flipped), 0.0)
        return carry

    lax.fori_loop(0, BINS, one, 0)
    for tile in range(0, DEPTH, 128):
        acc = jnp.zeros((ROWS, 128), jnp.float32)
        for place, i, low, high in pair_pieces():
            at = place - tile
            if 0 <= at < 128:
                moved = pltpu.roll(parts[i], (at - low) % 128, 1)
                acc = jnp.where((second >= at) & (second < at + high - low), moved, acc)
        width = min(128, DEPTH - tile)
        high = acc.astype(jnp.bfloat16)
        rest = (acc - high.astype(jnp.float32)).astype(jnp.bfloat16)
        matrix[0:ROWS, tile : tile + width] = high[:, :width]
        matrix[ROWS : 2 * ROWS, tile : tile + width] = rest[:, :width]


def kernel(
    size_x,
    size_y,
    mass_in,
    wind_x_in,
    wind_y_in,
    table_kernel,
    table_breakup,
    table_target,
    table_low,
    cloudy_in,
    out,
    mass,
    wind_x,
    wind_y,
    tables_f,
    tables_i,
    cloudy,
    state,
    last,
    moved,
    moved_last,
    coef,
    send_x,
    send_y,
    got_x,
    got_y,
    got_wx,
    got_wy,
    send_wy,
    padded,
    flipped,
    parts,
    matrix,
    products,
    change,
    sem_sx,
    sem_rx,
    sem_sy,
    sem_ry,
    sem_sw,
    sem_rw,
    sem_in,
):
    gx = lax.axis_index("gx")
    gy = lax.axis_index("gy")
    west = (lax.rem(gx + size_x - 1, size_x), gy)
    east = (lax.rem(gx + 1, size_x), gy)
    south = (gx, lax.rem(gy + size_y - 1, size_y))
    north = (gx, lax.rem(gy + 1, size_y))
    lane = lax.broadcasted_iota(jnp.int32, (CX, CY), 1)
    row = lax.broadcasted_iota(jnp.int32, (CX, CY), 0)
    wide = lax.broadcasted_iota(jnp.int32, (MAIN, CY), 1)

    def remote(src, dst, send, recv, device):
        return pltpu.make_async_remote_copy(
            src_ref=src, dst_ref=dst, send_sem=send, recv_sem=recv, device_id=device, device_id_type=MESH
        )

    def copies_x(stage, level):
        out = []
        far = lax.rem(gx, 2)
        for side in (far, 1 - far):
            device = (lax.rem(gx + size_x - 1 + 2 * side, size_x), gy)
            out.append(
                remote(
                    send_x.at[stage, level, side],
                    got_x.at[stage, level, 1 - side],
                    sem_sx.at[stage, level, side],
                    sem_rx.at[stage, level, 1 - side],
                    device,
                )
            )
        return out

    def copies_y(stage, level):
        out = []
        for side, device in ((1, north), (0, south)):
            out.append(
                remote(
                    send_y.at[stage, level, side],
                    got_y.at[stage, level, 1 - side],
                    sem_sy.at[stage, level, side],
                    sem_ry.at[stage, level, 1 - side],
                    device,
                )
            )
        return out

    def copies(stage, level):
        return copies_x(stage, level) + copies_y(stage, level)

    def wind_copies():
        return [
            remote(wind_x_in.at[pl.ds(24, 8)], got_wx, sem_sw.at[0], sem_rw.at[0], east),
            remote(send_wy, got_wy, sem_sw.at[1], sem_rw.at[1], north),
        ]

    def packed(pack, x, value):
        for j in range(4):
            at = 32 * j + 4 * x
            turned = pltpu.roll(value[8 * j : 8 * j + 8], (at - 126) % 128, 1)
            pack = jnp.where((lane >= at) & (lane < at + 4), turned, pack)
        return pack

    def keep_row(stage, level, x, value):
        state[stage, level, x] = value
        if x in OUTER:
            side, at = (0, x) if x < 2 else (1, x - (CX - 2))
            send_x[stage, level, side, at * MAIN : (at + 1) * MAIN] = value

    def keep_y(stage, level, pack, tail):
        send_y[stage, level, 0] = jnp.where(lane < 2, tail, pack)
        send_y[stage, level, 1] = jnp.where((lane >= 2) & (lane < 4), pltpu.roll(tail, 4, 1), pack)

    def keep(stage, level, values, tail):
        pack = jnp.zeros((CX, CY), jnp.float32)
        last[stage, level] = tail
        send_x[stage, level, 0, 2 * MAIN : EDGE] = tail[0:2]
        send_x[stage, level, 1, 2 * MAIN : EDGE] = tail[CX - 2 : CX]
        for x in OUTER:
            value = values(x)
            keep_row(stage, level, x, value)
            pack = packed(pack, x, value)
        for x in INNER:
            value = values(x)
            keep_row(stage, level, x, value)
            pack = packed(pack, x, value)
        keep_y(stage, level, pack, tail)
        for copy in copies_y(stage, level) + copies_x(stage, level):
            copy.start()

    barrier = pltpu.get_barrier_semaphore()
    for device in (west, east, south, north):
        pl.semaphore_signal(barrier, inc=1, device_id=device, device_id_type=MESH)

    span = BINS * LEVELS

    def rows_in(low, high, n):
        rows = pl.ds(low * span, (high - low) * span)
        return pltpu.make_async_copy(mass_in.at[rows], mass.at[rows], sem_in.at[n])

    mass_copies = [rows_in(0, 2, 0), rows_in(CX - 2, CX, 1), rows_in(2, CX - 2, 2)]
    others = [
        pltpu.make_async_copy(src, dst, sem_in.at[3 + n])
        for n, (src, dst) in enumerate(
            (
                (wind_x_in, wind_x),
                (wind_y_in, wind_y),
                (table_kernel, tables_f.at[0]),
                (table_breakup, tables_f.at[1]),
                (table_target, tables_i.at[0]),
                (table_low, tables_i.at[1]),
                (cloudy_in, cloudy),
            )
        )
    ]
    for copy in mass_copies + others:
        copy.start()
    for copy in mass_copies[:2]:
        copy.wait()

    def load_outer(level, carry):
        for x in OUTER:
            side, at = (0, x) if x < 2 else (1, x - (CX - 2))
            keep_row(0, level, x, mass[pl.ds(x * span + level, MAIN, stride=4), :])
            send_x[0, level, side, 2 * MAIN + at : 2 * MAIN + at + 1] = mass[pl.ds(x * span + 4 * MAIN + level, 1), :]
        return carry

    lax.fori_loop(0, LEVELS, load_outer, 0)

    others[1].wait()
    wind_pack = jnp.zeros((CX, CY), jnp.float32)
    for level in range(LEVELS):
        turned = wind_y[pl.ds(level, CX, stride=LEVELS), :]
        wind_pack = jnp.where(lane == CY - 1 - level, pltpu.roll(turned, (CY - level) % CY, 1), wind_pack)
    send_wy[...] = wind_pack
    pl.semaphore_wait(barrier, 4)
    for copy in wind_copies():
        copy.start()
    mass_copies[2].wait()

    def load_inner(level, carry):
        pack = jnp.zeros((CX, CY), jnp.float32)
        for x in INNER:
            keep_row(0, level, x, mass[pl.ds(x * span + level, MAIN, stride=4), :])
        for x in range(CX):
            pack = packed(pack, x, state[0, level, x])
        tail = mass[pl.ds(4 * MAIN + level, CX, stride=span), :]
        last[0, level] = tail
        keep_y(0, level, pack, tail)
        for copy in copies_y(0, level) + copies_x(0, level):
            copy.start()
        return carry

    lax.fori_loop(0, LEVELS, load_inner, 0)

    for copy in others[:1] + others[2:]:
        copy.wait()
    build_matrix((tables_f.at[0], tables_f.at[1], tables_i.at[0], tables_i.at[1]), padded, flipped, parts, matrix)

    flags = [cloudy[0, x] for x in range(CX)]
    count = jnp.int32(0)
    chosen = [jnp.int32(0)] * CAP
    slots = []
    for x in range(CX):
        slots.append(jnp.minimum(count, CAP - 1))
        for r in range(CAP):
            chosen[r] = jnp.where((flags[x] > 0) & (count == r), x, chosen[r])
        count = count + flags[x]
    live = [flags[x].astype(jnp.float32) for x in range(CX)]

    for copy in wind_copies():
        copy.wait_recv()

    def coefficients(level, carry):
        right = wind_x[pl.ds(level, CX, stride=LEVELS), :]
        left = jnp.where(row == 0, got_wx[pl.ds(4 + level, 1), :], pltpu.roll(right, 1, 0))
        above = wind_y[pl.ds(level, CX, stride=LEVELS), :]
        ghost = pltpu.roll(got_wy[...], level, 1)
        below = pltpu.roll(jnp.where(lane == CY - 1, ghost, above), 1, 1)

        def five(low, high):
            plus_low, minus_low = jnp.maximum(low, 0.0), jnp.minimum(low, 0.0)
            plus_high, minus_high = jnp.maximum(high, 0.0), jnp.minimum(high, 0.0)
            return (
                -0.5 * plus_low,
                1.5 * plus_low + 0.5 * plus_high,
                1.5 * minus_low - 1.5 * plus_high,
                -0.5 * minus_low - 1.5 * minus_high,
                0.5 * minus_high,
            )

        in_x = five(left, right)
        in_y = five(below, above)
        for n, value in enumerate(
            (in_x[0], in_x[1], in_x[3], in_x[4], in_y[0], in_y[1], in_y[3], in_y[4], 1.0 + (in_x[2] + in_y[2]))
        ):
            coef[level, n] = value
        return carry

    lax.fori_loop(0, LEVELS, coefficients, 0)

    def advance(stage, level):
        edge = jnp.where(lax.rem(lane, 4) < 2, got_y[stage, level, 0], got_y[stage, level, 1])

        def at_x(x):
            if x < 0:
                return got_x[stage, level, 0, (x + 2) * MAIN : (x + 3) * MAIN]
            if x >= CX:
                return got_x[stage, level, 1, (x - CX) * MAIN : (x - CX + 1) * MAIN]
            return state[stage, level, x]

        def value(x):
            c = [coef[level, n, x : x + 1, :] for n in range(9)]
            q = at_x(x)
            acc = c[8] * q
            acc += c[0] * at_x(x - 2) + c[1] * at_x(x - 1)
            acc += c[2] * at_x(x + 1) + c[3] * at_x(x + 2)
            ends = jnp.concatenate(
                [pltpu.roll(edge, (126 - 32 * j - 4 * x) % 128, 1) for j in range(4)], axis=0
            )
            acc += c[4] * pltpu.roll(jnp.where(wide >= CY - 2, ends, q), 2, 1)
            acc += c[5] * pltpu.roll(jnp.where(wide >= CY - 1, ends, q), 1, 1)
            acc += c[6] * pltpu.roll(jnp.where(wide < 1, ends, q), CY - 1, 1)
            acc += c[7] * pltpu.roll(jnp.where(wide < 2, ends, q), CY - 2, 1)
            return acc

        c = [coef[level, n] for n in range(9)]
        e = last[stage, level]
        below_x = jnp.where(
            row == CX - 1,
            got_x[stage, level, 0, 2 * MAIN + 1 : 2 * MAIN + 2],
            got_x[stage, level, 0, 2 * MAIN : 2 * MAIN + 1],
        )
        above_x = jnp.where(
            row == 0,
            got_x[stage, level, 1, 2 * MAIN : 2 * MAIN + 1],
            got_x[stage, level, 1, 2 * MAIN + 1 : 2 * MAIN + 2],
        )
        below_y = pltpu.roll(got_y[stage, level, 0], CY - 4, 1)
        above_y = got_y[stage, level, 1]
        acc = c[8] * e
        acc += c[0] * pltpu.roll(jnp.where(row >= CX - 2, below_x, e), 2, 0)
        acc += c[1] * pltpu.roll(jnp.where(row >= CX - 1, below_x, e), 1, 0)
        acc += c[2] * pltpu.roll(jnp.where(row < 1, above_x, e), CX - 1, 0)
        acc += c[3] * pltpu.roll(jnp.where(row < 2, above_x, e), CX - 2, 0)
        acc += c[4] * pltpu.roll(jnp.where(lane >= CY - 2, below_y, e), 2, 1)
        acc += c[5] * pltpu.roll(jnp.where(lane >= CY - 1, below_y, e), 1, 1)
        acc += c[6] * pltpu.roll(jnp.where(lane < 1, above_y, e), CY - 1, 1)
        acc += c[7] * pltpu.roll(jnp.where(lane < 2, above_y, e), CY - 2, 1)
        return value, acc

    def collide():
        for r in range(CAP):
            x = chosen[r]
            cols = slice(r * CY, (r + 1) * CY)
            n = moved[x]
            e = moved_last[pl.ds(x, 1), :]

            def bin_of(i):
                return moved[x, i : i + 1, :]

            for a in range(8):
                products[32 * a : 32 * a + 32, cols] = (bin_of(a) * n).astype(jnp.bfloat16)
                products[32 * (8 + a) : 32 * (9 + a), cols] = jnp.concatenate(
                    [bin_of(24 + a) * n[24:32], bin_of(8 + a) * n[8:32]], axis=0
                ).astype(jnp.bfloat16)
            for a in range(4):
                products[32 * (16 + a) : 32 * (17 + a), cols] = jnp.concatenate(
                    [bin_of(20 + a) * n[16:32], bin_of(16 + a) * n[16:32]], axis=0
                ).astype(jnp.bfloat16)
            products[640:672, cols] = (e * n).astype(jnp.bfloat16)
            products[672:688, cols] = jnp.broadcast_to(e * e, (16, CY)).astype(jnp.bfloat16)
        result = jnp.dot(matrix[...], products[...], preferred_element_type=jnp.float32)
        for r in range(CAP):
            cols = slice(r * CY, (r + 1) * CY)
            change[r] = result[0:ROWS, cols] + result[ROWS : 2 * ROWS, cols]

    for copy in wind_copies():
        copy.wait_send()

    for stage in range(STAGES):

        def step(level, carry, stage=stage):
            for copy in copies(stage - 1, level) if stage else []:
                copy.wait_send()
            for copy in copies(stage, level):
                copy.wait_recv()
            for copy in copies(stage, level) if stage == STAGES - 1 else []:
                copy.wait_send()
            value, tail = advance(stage, level)
            if stage % 2 == 0:
                keep(stage + 1, level, value, tail)
            else:
                for x in range(CX):
                    moved[x] = 0.5 * state[stage - 1, level, x] + 0.5 * value(x)
                moved_last[...] = 0.5 * last[stage - 1, level] + 0.5 * tail
                collide()

                def after(x):
                    return moved[x] + live[x] * change[slots[x], 0:MAIN]

                for x in range(CX):
                    moved_last[x : x + 1, :] = (
                        moved_last[x : x + 1, :] + live[x] * change[slots[x], MAIN : MAIN + 1]
                    )
                tail = moved_last[...]
                if stage < STAGES - 1:
                    keep(stage + 1, level, after, tail)
                else:
                    for x in range(CX):
                        out[pl.ds(x * 4 * BINS + level, MAIN, stride=4), :] = after(x)
                    out[pl.ds(4 * MAIN + level, CX, stride=4 * BINS), :] = tail
            return carry

        lax.fori_loop(0, LEVELS, step, 0)


def local(size_x, size_y, droplet_mass, wind_x, wind_y, table, breakup, target, fragment_low, cloudy):
    vmem = pl.BlockSpec(memory_space=pltpu.VMEM)
    f32 = jnp.float32
    result = pl.pallas_call(
        functools.partial(kernel, size_x, size_y),
        out_shape=pltpu.VMEM((CX * BINS * LEVELS, CY), f32),
        in_specs=[pl.BlockSpec(memory_space=pltpu.HBM)] * 8,
        out_specs=vmem,
        scratch_shapes=[
            pltpu.VMEM((CX * BINS * LEVELS, CY), f32),
            pltpu.VMEM((CX * LEVELS, CY), f32),
            pltpu.VMEM((CX * LEVELS, CY), f32),
            pltpu.VMEM((2, BINS, BINS), f32),
            pltpu.VMEM((2, BINS, BINS), jnp.int32),
            pltpu.SMEM((1, CX), jnp.int32),
            pltpu.VMEM((STAGES, LEVELS, CX, MAIN, CY), f32),
            pltpu.VMEM((STAGES, LEVELS, CX, CY), f32),
            pltpu.VMEM((CX, MAIN, CY), f32),
            pltpu.VMEM((CX, CY), f32),
            pltpu.VMEM((LEVELS, 9, CX, CY), f32),
            pltpu.VMEM((STAGES, LEVELS, 2, EDGE, CY), f32),
            pltpu.VMEM((STAGES, LEVELS, 2, CX, CY), f32),
            pltpu.VMEM((STAGES, LEVELS, 2, EDGE, CY), f32),
            pltpu.VMEM((STAGES, LEVELS, 2, CX, CY), f32),
            pltpu.VMEM((8, CY), f32),
            pltpu.VMEM((CX, CY), f32),
            pltpu.VMEM((CX, CY), f32),
            pltpu.VMEM((4, 128, 128), f32),
            pltpu.VMEM((4, 128, 128), f32),
            pltpu.VMEM((BINS, ROWS, 128), f32),
            pltpu.VMEM((2 * ROWS, DEPTH), jnp.bfloat16),
            pltpu.VMEM((DEPTH, CAP * CY), jnp.bfloat16),
            pltpu.VMEM((CAP, ROWS, CY), f32),
            pltpu.SemaphoreType.DMA((STAGES, LEVELS, 2)),
            pltpu.SemaphoreType.DMA((STAGES, LEVELS, 2)),
            pltpu.SemaphoreType.DMA((STAGES, LEVELS, 2)),
            pltpu.SemaphoreType.DMA((STAGES, LEVELS, 2)),
            pltpu.SemaphoreType.DMA((2,)),
            pltpu.SemaphoreType.DMA((2,)),
            pltpu.SemaphoreType.DMA((10,)),
        ],
        compiler_params=pltpu.CompilerParams(
            collective_id=0, has_side_effects=True, vmem_limit_bytes=58 * 2**20
        ),
    )(
        droplet_mass.reshape(CX * BINS * LEVELS, CY),
        wind_x.reshape(CX * LEVELS, CY),
        wind_y.reshape(CX * LEVELS, CY),
        table,
        breakup,
        target,
        fragment_low,
        cloudy.reshape(1, CX),
    )
    return result.reshape(CX, BINS, LEVELS, CY)


def solution(mesh):
    in_specs = (
        P("gx", None, None, "gy"),
        P("gx", None, "gy"),
        P("gx", None, "gy"),
        P(),
        P(),
        P(),
        P(),
        P("gx", "gy"),
    )
    return jax.shard_map(
        functools.partial(local, mesh.shape["gx"], mesh.shape["gy"]),
        mesh=mesh,
        in_specs=in_specs,
        out_specs=P("gx", None, None, "gy"),
        check_vma=False,
    )
```

```python
import functools

import jax
import jax.numpy as jnp
from jax import lax
from jax.experimental import pallas as pl
from jax.experimental.pallas import tpu as pltpu
from jax.sharding import PartitionSpec as P

STEPS = 2
STAGES = 2 * STEPS
BINS = 33
MAIN = 32
LEVELS = 4
CX = 8
CY = 128
CAP = 4
DEPTH = 688
ROWS = 48
EDGE = 2 * MAIN + 2
OUTER = (0, 1, CX - 2, CX - 1)
INNER = tuple(range(2, CX - 2))
MESH = pl.DeviceIdType.MESH


def pair_pieces():
    pieces = []
    for a in range(8):
        pieces.append((32 * a, a, 0, 32))
        pieces.append((32 * (8 + a), 24 + a, 24, 32))
        pieces.append((32 * (8 + a) + 8, 8 + a, 8, 32))
    for a in range(4):
        pieces.append((32 * (16 + a), 20 + a, 16, 32))
        pieces.append((32 * (16 + a) + 16, 16 + a, 16, 32))
    pieces.append((32 * 20, 32, 0, 32))
    pieces.append((32 * 21, 32, 32, 33))
    return pieces


def build_matrix(tables, padded, flipped, parts, matrix):
    for n, table in enumerate(tables):
        padded[n] = jnp.zeros((128, 128), jnp.float32)
        padded[n, 0:BINS, 0:BINS] = table[...].astype(jnp.float32)
        flipped[n] = padded[n].T
    out_bin = lax.broadcasted_iota(jnp.int32, (ROWS, 128), 0).astype(jnp.float32)
    second = lax.broadcasted_iota(jnp.int32, (ROWS, 128), 1)
    lanes = lax.broadcasted_iota(jnp.int32, (1, 128), 1)

    def one(i, carry):
        first = jnp.full((1, 128), i, jnp.int32).astype(jnp.float32)
        larger = jnp.maximum(first, lanes.astype(jnp.float32))
        losses = 0.5 * jnp.where(out_bin == first, 1.0, 0.0) + 0.5 * jnp.where(
            out_bin == second.astype(jnp.float32), 1.0, 0.0
        )

        def rates(source):
            kern, brk, tgt, low = (source[n, pl.ds(i, 1), :] for n in range(4))
            each = brk * (1.0 / (larger - low + 1.0))
            merged = jnp.where(out_bin == tgt, 1.0 - brk, 0.0)
            broken = jnp.where((out_bin >= low) & (out_bin <= larger), each, 0.0)
            rounded = (kern * (merged + broken - losses)).astype(jnp.bfloat16)
            return rounded.astype(jnp.float32)

        start = jnp.where(i == MAIN, 0, (i // 8) * 8 + 8)
        end = jnp.where(i == MAIN, MAIN, BINS)
        both = (second >= start) & (second < end)
        parts[i] = rates(padded) + jnp.where(both, rates(flipped), 0.0)
        return carry

    lax.fori_loop(0, BINS, one, 0)
    for tile in range(0, DEPTH, 128):
        acc = jnp.zeros((ROWS, 128), jnp.float32)
        for place, i, low, high in pair_pieces():
            at = place - tile
            if 0 <= at < 128:
                moved = pltpu.roll(parts[i], (at - low) % 128, 1)
                acc = jnp.where((second >= at) & (second < at + high - low), moved, acc)
        width = min(128, DEPTH - tile)
        high = acc.astype(jnp.bfloat16)
        rest = (acc - high.astype(jnp.float32)).astype(jnp.bfloat16)
        matrix[0:ROWS, tile : tile + width] = high[:, :width]
        matrix[ROWS : 2 * ROWS, tile : tile + width] = rest[:, :width]


def kernel(
    size_x,
    size_y,
    mass_in,
    wind_x_in,
    wind_y_in,
    table_kernel,
    table_breakup,
    table_target,
    table_low,
    cloudy_in,
    out,
    mass,
    wind_x,
    wind_y,
    tables_f,
    tables_i,
    cloudy,
    state,
    last,
    moved,
    moved_last,
    coef,
    send_x,
    send_y,
    got_x,
    got_y,
    got_wx,
    got_wy,
    send_wy,
    padded,
    flipped,
    parts,
    matrix,
    products,
    change,
    sem_sx,
    sem_rx,
    sem_sy,
    sem_ry,
    sem_sw,
    sem_rw,
    sem_in,
):
    gx = lax.axis_index("gx")
    gy = lax.axis_index("gy")
    west = (lax.rem(gx + size_x - 1, size_x), gy)
    east = (lax.rem(gx + 1, size_x), gy)
    south = (gx, lax.rem(gy + size_y - 1, size_y))
    north = (gx, lax.rem(gy + 1, size_y))
    lane = lax.broadcasted_iota(jnp.int32, (CX, CY), 1)
    row = lax.broadcasted_iota(jnp.int32, (CX, CY), 0)
    wide = lax.broadcasted_iota(jnp.int32, (MAIN, CY), 1)

    def remote(src, dst, send, recv, device):
        return pltpu.make_async_remote_copy(
            src_ref=src, dst_ref=dst, send_sem=send, recv_sem=recv, device_id=device, device_id_type=MESH
        )

    def copies_x(stage, level):
        out = []
        far = lax.rem(gx, 2)
        for side in (far, 1 - far):
            device = (lax.rem(gx + size_x - 1 + 2 * side, size_x), gy)
            out.append(
                remote(
                    send_x.at[stage, level, side],
                    got_x.at[stage, level, 1 - side],
                    sem_sx.at[stage, level, side],
                    sem_rx.at[stage, level, 1 - side],
                    device,
                )
            )
        return out

    def copies_y(stage, level):
        out = []
        for side, device in ((1, north), (0, south)):
            out.append(
                remote(
                    send_y.at[stage, level, side],
                    got_y.at[stage, level, 1 - side],
                    sem_sy.at[stage, level, side],
                    sem_ry.at[stage, level, 1 - side],
                    device,
                )
            )
        return out

    def copies(stage, level):
        return copies_x(stage, level) + copies_y(stage, level)

    def wind_copies():
        return [
            remote(wind_x_in.at[pl.ds(24, 8)], got_wx, sem_sw.at[0], sem_rw.at[0], east),
            remote(send_wy, got_wy, sem_sw.at[1], sem_rw.at[1], north),
        ]

    def packed(pack, x, value):
        for j in range(4):
            at = 32 * j + 4 * x
            turned = pltpu.roll(value[8 * j : 8 * j + 8], (at - 126) % 128, 1)
            pack = jnp.where((lane >= at) & (lane < at + 4), turned, pack)
        return pack

    def keep_row(stage, level, x, value):
        state[stage, level, x] = value
        if x in OUTER:
            side, at = (0, x) if x < 2 else (1, x - (CX - 2))
            send_x[stage, level, side, at * MAIN : (at + 1) * MAIN] = value

    def keep_y(stage, level, pack, tail):
        send_y[stage, level, 0] = jnp.where(lane < 2, tail, pack)
        send_y[stage, level, 1] = jnp.where((lane >= 2) & (lane < 4), pltpu.roll(tail, 4, 1), pack)

    def keep(stage, level, values, tail):
        pack = jnp.zeros((CX, CY), jnp.float32)
        last[stage, level] = tail
        send_x[stage, level, 0, 2 * MAIN : EDGE] = tail[0:2]
        send_x[stage, level, 1, 2 * MAIN : EDGE] = tail[CX - 2 : CX]
        for x in OUTER:
            value = values(x)
            keep_row(stage, level, x, value)
            pack = packed(pack, x, value)
        for x in INNER:
            value = values(x)
            keep_row(stage, level, x, value)
            pack = packed(pack, x, value)
        keep_y(stage, level, pack, tail)
        for copy in copies_x(stage, level)[:1] + copies_y(stage, level) + copies_x(stage, level)[1:]:
            copy.start()

    barrier = pltpu.get_barrier_semaphore()
    for device in (west, east, south, north):
        pl.semaphore_signal(barrier, inc=1, device_id=device, device_id_type=MESH)

    span = BINS * LEVELS

    def rows_in(low, high, n):
        rows = pl.ds(low * span, (high - low) * span)
        return pltpu.make_async_copy(mass_in.at[rows], mass.at[rows], sem_in.at[n])

    mass_copies = [rows_in(0, 2, 0), rows_in(CX - 2, CX, 1), rows_in(2, CX - 2, 2)]
    others = [
        pltpu.make_async_copy(src, dst, sem_in.at[3 + n])
        for n, (src, dst) in enumerate(
            (
                (wind_x_in, wind_x),
                (wind_y_in, wind_y),
                (table_kernel, tables_f.at[0]),
                (table_breakup, tables_f.at[1]),
                (table_target, tables_i.at[0]),
                (table_low, tables_i.at[1]),
                (cloudy_in, cloudy),
            )
        )
    ]
    for copy in mass_copies + others:
        copy.start()
    for copy in mass_copies[:2]:
        copy.wait()

    def load_outer(level, carry):
        for x in OUTER:
            side, at = (0, x) if x < 2 else (1, x - (CX - 2))
            keep_row(0, level, x, mass[pl.ds(x * span + level, MAIN, stride=4), :])
            send_x[0, level, side, 2 * MAIN + at : 2 * MAIN + at + 1] = mass[pl.ds(x * span + 4 * MAIN + level, 1), :]
        return carry

    lax.fori_loop(0, LEVELS, load_outer, 0)

    others[1].wait()
    wind_pack = jnp.zeros((CX, CY), jnp.float32)
    for level in range(LEVELS):
        turned = wind_y[pl.ds(level, CX, stride=LEVELS), :]
        wind_pack = jnp.where(lane == CY - 1 - level, pltpu.roll(turned, (CY - level) % CY, 1), wind_pack)
    send_wy[...] = wind_pack
    pl.semaphore_wait(barrier, 4)
    for copy in wind_copies():
        copy.start()
    mass_copies[2].wait()

    def load_inner(level, carry):
        pack = jnp.zeros((CX, CY), jnp.float32)
        for x in INNER:
            keep_row(0, level, x, mass[pl.ds(x * span + level, MAIN, stride=4), :])
        for x in range(CX):
            pack = packed(pack, x, state[0, level, x])
        tail = mass[pl.ds(4 * MAIN + level, CX, stride=span), :]
        last[0, level] = tail
        keep_y(0, level, pack, tail)
        for copy in copies_y(0, level) + copies_x(0, level):
            copy.start()
        return carry

    lax.fori_loop(0, LEVELS, load_inner, 0)

    for copy in others[:1] + others[2:]:
        copy.wait()
    build_matrix((tables_f.at[0], tables_f.at[1], tables_i.at[0], tables_i.at[1]), padded, flipped, parts, matrix)

    flags = [cloudy[0, x] for x in range(CX)]
    count = jnp.int32(0)
    chosen = [jnp.int32(0)] * CAP
    slots = []
    for x in range(CX):
        slots.append(jnp.minimum(count, CAP - 1))
        for r in range(CAP):
            chosen[r] = jnp.where((flags[x] > 0) & (count == r), x, chosen[r])
        count = count + flags[x]
    live = [flags[x].astype(jnp.float32) for x in range(CX)]

    for copy in wind_copies():
        copy.wait_recv()

    def coefficients(level, carry):
        right = wind_x[pl.ds(level, CX, stride=LEVELS), :]
        left = jnp.where(row == 0, got_wx[pl.ds(4 + level, 1), :], pltpu.roll(right, 1, 0))
        above = wind_y[pl.ds(level, CX, stride=LEVELS), :]
        ghost = pltpu.roll(got_wy[...], level, 1)
        below = pltpu.roll(jnp.where(lane == CY - 1, ghost, above), 1, 1)

        def five(low, high):
            plus_low, minus_low = jnp.maximum(low, 0.0), jnp.minimum(low, 0.0)
            plus_high, minus_high = jnp.maximum(high, 0.0), jnp.minimum(high, 0.0)
            return (
                -0.5 * plus_low,
                1.5 * plus_low + 0.5 * plus_high,
                1.5 * minus_low - 1.5 * plus_high,
                -0.5 * minus_low - 1.5 * minus_high,
                0.5 * minus_high,
            )

        in_x = five(left, right)
        in_y = five(below, above)
        for n, value in enumerate(
            (in_x[0], in_x[1], in_x[3], in_x[4], in_y[0], in_y[1], in_y[3], in_y[4], 1.0 + (in_x[2] + in_y[2]))
        ):
            coef[level, n] = value
        return carry

    lax.fori_loop(0, LEVELS, coefficients, 0)

    def advance(stage, level):
        edge = jnp.where(lax.rem(lane, 4) < 2, got_y[stage, level, 0], got_y[stage, level, 1])

        def at_x(x):
            if x < 0:
                return got_x[stage, level, 0, (x + 2) * MAIN : (x + 3) * MAIN]
            if x >= CX:
                return got_x[stage, level, 1, (x - CX) * MAIN : (x - CX + 1) * MAIN]
            return state[stage, level, x]

        def value(x):
            c = [coef[level, n, x : x + 1, :] for n in range(9)]
            q = at_x(x)
            acc = c[8] * q
            acc += c[0] * at_x(x - 2) + c[1] * at_x(x - 1)
            acc += c[2] * at_x(x + 1) + c[3] * at_x(x + 2)
            ends = jnp.concatenate(
                [pltpu.roll(edge, (126 - 32 * j - 4 * x) % 128, 1) for j in range(4)], axis=0
            )
            acc += c[4] * pltpu.roll(jnp.where(wide >= CY - 2, ends, q), 2, 1)
            acc += c[5] * pltpu.roll(jnp.where(wide >= CY - 1, ends, q), 1, 1)
            acc += c[6] * pltpu.roll(jnp.where(wide < 1, ends, q), CY - 1, 1)
            acc += c[7] * pltpu.roll(jnp.where(wide < 2, ends, q), CY - 2, 1)
            return acc

        c = [coef[level, n] for n in range(9)]
        e = last[stage, level]
        below_x = jnp.where(
            row == CX - 1,
            got_x[stage, level, 0, 2 * MAIN + 1 : 2 * MAIN + 2],
            got_x[stage, level, 0, 2 * MAIN : 2 * MAIN + 1],
        )
        above_x = jnp.where(
            row == 0,
            got_x[stage, level, 1, 2 * MAIN : 2 * MAIN + 1],
            got_x[stage, level, 1, 2 * MAIN + 1 : 2 * MAIN + 2],
        )
        below_y = pltpu.roll(got_y[stage, level, 0], CY - 4, 1)
        above_y = got_y[stage, level, 1]
        acc = c[8] * e
        acc += c[0] * pltpu.roll(jnp.where(row >= CX - 2, below_x, e), 2, 0)
        acc += c[1] * pltpu.roll(jnp.where(row >= CX - 1, below_x, e), 1, 0)
        acc += c[2] * pltpu.roll(jnp.where(row < 1, above_x, e), CX - 1, 0)
        acc += c[3] * pltpu.roll(jnp.where(row < 2, above_x, e), CX - 2, 0)
        acc += c[4] * pltpu.roll(jnp.where(lane >= CY - 2, below_y, e), 2, 1)
        acc += c[5] * pltpu.roll(jnp.where(lane >= CY - 1, below_y, e), 1, 1)
        acc += c[6] * pltpu.roll(jnp.where(lane < 1, above_y, e), CY - 1, 1)
        acc += c[7] * pltpu.roll(jnp.where(lane < 2, above_y, e), CY - 2, 1)
        return value, acc

    def collide():
        for r in range(CAP):
            x = chosen[r]
            cols = slice(r * CY, (r + 1) * CY)
            n = moved[x]
            e = moved_last[pl.ds(x, 1), :]

            def bin_of(i):
                return moved[x, i : i + 1, :]

            for a in range(8):
                products[32 * a : 32 * a + 32, cols] = (bin_of(a) * n).astype(jnp.bfloat16)
                products[32 * (8 + a) : 32 * (9 + a), cols] = jnp.concatenate(
                    [bin_of(24 + a) * n[24:32], bin_of(8 + a) * n[8:32]], axis=0
                ).astype(jnp.bfloat16)
            for a in range(4):
                products[32 * (16 + a) : 32 * (17 + a), cols] = jnp.concatenate(
                    [bin_of(20 + a) * n[16:32], bin_of(16 + a) * n[16:32]], axis=0
                ).astype(jnp.bfloat16)
            products[640:672, cols] = (e * n).astype(jnp.bfloat16)
            products[672:688, cols] = jnp.broadcast_to(e * e, (16, CY)).astype(jnp.bfloat16)
        result = jnp.dot(matrix[...], products[...], preferred_element_type=jnp.float32)
        for r in range(CAP):
            cols = slice(r * CY, (r + 1) * CY)
            change[r] = result[0:ROWS, cols] + result[ROWS : 2 * ROWS, cols]

    for copy in wind_copies():
        copy.wait_send()

    for stage in range(STAGES):

        def step(level, carry, stage=stage):
            for copy in copies(stage - 1, level) if stage else []:
                copy.wait_send()
            for copy in copies(stage, level):
                copy.wait_recv()
            for copy in copies(stage, level) if stage == STAGES - 1 else []:
                copy.wait_send()
            value, tail = advance(stage, level)
            if stage % 2 == 0:
                keep(stage + 1, level, value, tail)
            else:
                for x in range(CX):
                    moved[x] = 0.5 * state[stage - 1, level, x] + 0.5 * value(x)
                moved_last[...] = 0.5 * last[stage - 1, level] + 0.5 * tail
                collide()

                def after(x):
                    return moved[x] + live[x] * change[slots[x], 0:MAIN]

                for x in range(CX):
                    moved_last[x : x + 1, :] = (
                        moved_last[x : x + 1, :] + live[x] * change[slots[x], MAIN : MAIN + 1]
                    )
                tail = moved_last[...]
                if stage < STAGES - 1:
                    keep(stage + 1, level, after, tail)
                else:
                    for x in range(CX):
                        out[pl.ds(x * 4 * BINS + level, MAIN, stride=4), :] = after(x)
                    out[pl.ds(4 * MAIN + level, CX, stride=4 * BINS), :] = tail
            return carry

        lax.fori_loop(0, LEVELS, step, 0)


def local(size_x, size_y, droplet_mass, wind_x, wind_y, table, breakup, target, fragment_low, cloudy):
    vmem = pl.BlockSpec(memory_space=pltpu.VMEM)
    f32 = jnp.float32
    result = pl.pallas_call(
        functools.partial(kernel, size_x, size_y),
        out_shape=pltpu.VMEM((CX * BINS * LEVELS, CY), f32),
        in_specs=[pl.BlockSpec(memory_space=pltpu.HBM)] * 8,
        out_specs=vmem,
        scratch_shapes=[
            pltpu.VMEM((CX * BINS * LEVELS, CY), f32),
            pltpu.VMEM((CX * LEVELS, CY), f32),
            pltpu.VMEM((CX * LEVELS, CY), f32),
            pltpu.VMEM((2, BINS, BINS), f32),
            pltpu.VMEM((2, BINS, BINS), jnp.int32),
            pltpu.SMEM((1, CX), jnp.int32),
            pltpu.VMEM((STAGES, LEVELS, CX, MAIN, CY), f32),
            pltpu.VMEM((STAGES, LEVELS, CX, CY), f32),
            pltpu.VMEM((CX, MAIN, CY), f32),
            pltpu.VMEM((CX, CY), f32),
            pltpu.VMEM((LEVELS, 9, CX, CY), f32),
            pltpu.VMEM((STAGES, LEVELS, 2, EDGE, CY), f32),
            pltpu.VMEM((STAGES, LEVELS, 2, CX, CY), f32),
            pltpu.VMEM((STAGES, LEVELS, 2, EDGE, CY), f32),
            pltpu.VMEM((STAGES, LEVELS, 2, CX, CY), f32),
            pltpu.VMEM((8, CY), f32),
            pltpu.VMEM((CX, CY), f32),
            pltpu.VMEM((CX, CY), f32),
            pltpu.VMEM((4, 128, 128), f32),
            pltpu.VMEM((4, 128, 128), f32),
            pltpu.VMEM((BINS, ROWS, 128), f32),
            pltpu.VMEM((2 * ROWS, DEPTH), jnp.bfloat16),
            pltpu.VMEM((DEPTH, CAP * CY), jnp.bfloat16),
            pltpu.VMEM((CAP, ROWS, CY), f32),
            pltpu.SemaphoreType.DMA((STAGES, LEVELS, 2)),
            pltpu.SemaphoreType.DMA((STAGES, LEVELS, 2)),
            pltpu.SemaphoreType.DMA((STAGES, LEVELS, 2)),
            pltpu.SemaphoreType.DMA((STAGES, LEVELS, 2)),
            pltpu.SemaphoreType.DMA((2,)),
            pltpu.SemaphoreType.DMA((2,)),
            pltpu.SemaphoreType.DMA((10,)),
        ],
        compiler_params=pltpu.CompilerParams(
            collective_id=0, has_side_effects=True, vmem_limit_bytes=58 * 2**20
        ),
    )(
        droplet_mass.reshape(CX * BINS * LEVELS, CY),
        wind_x.reshape(CX * LEVELS, CY),
        wind_y.reshape(CX * LEVELS, CY),
        table,
        breakup,
        target,
        fragment_low,
        cloudy.reshape(1, CX),
    )
    return result.reshape(CX, BINS, LEVELS, CY)


def solution(mesh):
    in_specs = (
        P("gx", None, None, "gy"),
        P("gx", None, "gy"),
        P("gx", None, "gy"),
        P(),
        P(),
        P(),
        P(),
        P("gx", "gy"),
    )
    return jax.shard_map(
        functools.partial(local, mesh.shape["gx"], mesh.shape["gy"]),
        mesh=mesh,
        in_specs=in_specs,
        out_specs=P("gx", None, None, "gy"),
        check_vma=False,
    )
```
